256 devices in a mesh: row: 4 (over z_hi), col: 8 (over y, core), dep: 8 (over z_lo, x).
Axes of the slice: x: 4, y: 4, z: 8 (z_hi: 4, z_lo: 2; z = z_hi * 2 + z_lo), core: 2. Of those that a mesh axis runs over, the one named last changes fastest.
Arguments:
- activations: bfloat16 [512, 5120], P(('col', 'dep'), 'row'), may hold values from -30 to 30
- out_weight: bfloat16 [5120, 151936], P('row', ('col', 'dep')), may hold values from -1 to 1
- teacher_ids: int32 [512, 64], replicated, may hold values from 0 to 151935, as said below
- teacher_values: float32 [512, 64], replicated, may hold values from -8 to 310
Outputs:
- grad_activations: bfloat16 [512, 5120], P(('col', 'dep'), 'row')
- grad_weight: bfloat16 [5120, 151936], P('row', ('col', 'dep'))
The draws below stay inside these ranges and needn't reach their ends.
Inputs may be any that keep to these rules, and one draw needn't show every extreme that they name: `teacher_ids`: each row names 64 different token ids.
All inputs are finite; a program needn't handle non-finite values.
Results may differ from the reference program's by a relative error of at most 0.0046.
Values may be sent and summed in bfloat16 or wider, within the bound.
No kernel may reach another device: no remote copies, remote signals or barrier semaphores. Data moves between devices by JAX's collectives and lax.ppermute only.
A program may use at most 128 MiB of HBM per device.

```python
import math
import jax
import jax.numpy as jnp

D = 5120
V = 151936
K = 64
TOKENS = 512


def base_states(key):
    key_one, key_two = jax.random.split(key)
    unit_rows = jnp.clip(jax.random.normal(key_one, (TOKENS, D), jnp.float32), -6.0, 6.0)
    scales = jnp.exp(jax.random.uniform(key_two, (TOKENS, 1), jnp.float32, math.log(0.5), math.log(5.0)))
    return (unit_rows, scales)


def draw_activations(key, part):
    unit_rows, scales = base_states(key)
    return (unit_rows * scales).astype(jnp.bfloat16)


def draw_out_weight(key, part):
    key = jax.random.fold_in(key, 7)
    spread_scale = 3.0 / math.sqrt(D)
    weights = jnp.clip(jax.random.normal(key, (D, V), jnp.float32), -6.0, 6.0) * spread_scale
    return weights.astype(jnp.bfloat16)


def draw_teacher_ids(key, part):
    key = jax.random.fold_in(key, 11)
    subkeys = jax.random.split(key, 3)
    gap_sizes = jax.random.randint(subkeys[0], (TOKENS, K), 1, V // K + 1)
    offsets = jnp.cumsum(gap_sizes, axis=1) - gap_sizes[:, :1]
    start_ids = jax.random.randint(subkeys[1], (TOKENS, 1), 0, V)
    start_ids = start_ids.at[0, 0].set(V - 1).at[1, 0].set(0)
    token_ids = (start_ids + offsets) % V
    token_ids = jax.random.permutation(subkeys[2], token_ids, axis=1, independent=True)
    return token_ids.astype(jnp.int32)


def draw_teacher_values(key, part):
    key = jax.random.fold_in(key, 13)
    key_one = jax.random.fold_in(key, 0)
    values = jnp.clip(2.0 * jax.random.normal(key_one, (TOKENS, K), jnp.float32), -8.0, 8.0)
    return values


def setup_inputs(seed: int = 0) -> dict:
    streams_of = jax.random.split(jax.random.key(seed), 5)
    activations = draw_activations(jax.random.fold_in(streams_of[4], 71), 0)
    out_weight = draw_out_weight(jax.random.fold_in(streams_of[4], 71), 0)
    teacher_ids = draw_teacher_ids(jax.random.fold_in(streams_of[4], 71), 0)
    teacher_values = draw_teacher_values(jax.random.fold_in(streams_of[4], 71), 0)
    return {"activations": activations, "out_weight": out_weight, "teacher_ids": teacher_ids, "teacher_values": teacher_values}


loss_scale = 64.0


def reference(activations, out_weight, teacher_ids, teacher_values):
    logits = jnp.dot(activations, out_weight, preferred_element_type=jnp.float32)
    row_peak = jnp.max(logits, axis=1, keepdims=True)
    shifted_exp = jnp.exp(logits - row_peak)
    row_total = jnp.sum(shifted_exp, axis=1, keepdims=True)
    student = shifted_exp / row_total
    teacher_peak = jnp.max(teacher_values, axis=1, keepdims=True)
    teacher_exp = jnp.exp(teacher_values - teacher_peak)
    teacher = teacher_exp / jnp.sum(teacher_exp, axis=1, keepdims=True)
    row_index = jnp.broadcast_to(jnp.arange(TOKENS, dtype=jnp.int32)[:, None], teacher_ids.shape)
    teacher_dense = jnp.zeros(logits.shape, jnp.float32).at[row_index, teacher_ids].add(teacher)
    grad_logits = (loss_scale * (student - teacher_dense)).astype(jnp.bfloat16)
    grad_activations = jnp.dot(grad_logits, out_weight.T, preferred_element_type=jnp.float32).astype(jnp.bfloat16)
    grad_weight = jnp.dot(activations.T, grad_logits, preferred_element_type=jnp.float32).astype(jnp.bfloat16)
    return (grad_activations, grad_weight)
```

```python
import functools

import jax
import jax.numpy as jnp
from jax import lax
from jax.experimental import pallas as pl
from jax.experimental.pallas import tpu as pltpu
from jax.sharding import Mesh, PartitionSpec as P

LOSS_SCALE = 64.0
CODE_SCALE = 65535.0
CODE_OFFSET = 32768.0
F32 = jnp.float32
BF16 = jnp.bfloat16
I16 = jnp.int16
I32 = jnp.int32
VMEM = pl.BlockSpec(memory_space=pltpu.VMEM)
SMEM = pl.BlockSpec(memory_space=pltpu.SMEM)
PARAMS = pltpu.CompilerParams(vmem_limit_bytes=20 * 1024 * 1024)
CHIP = ("y", "z_lo", "x")
SHARD = ("y", "core", "z_lo", "x")


def cost(flops, bytes_accessed, exps=0):
    return pl.CostEstimate(flops=flops, bytes_accessed=bytes_accessed, transcendentals=exps)


def lanes_of(shape):
    return lax.broadcasted_iota(I32, shape, 1)


def encode(x, width):
    lane = lanes_of(x.shape)
    inside = lane < width
    high = jnp.max(jnp.where(inside, x, -jnp.inf), axis=1, keepdims=True)
    low = jnp.min(jnp.where(inside, x, jnp.inf), axis=1, keepdims=True)
    size = jnp.maximum(jnp.abs(high), jnp.abs(low))
    step = jnp.maximum(jnp.maximum((high - low) * (1.0 / 65000.0), size * 2.0**-22), 1e-30)
    power = jnp.ceil(jnp.log2(step))
    inverse = jnp.exp2(-power)
    middle = jnp.round((0.5 * high + 0.5 * low) * inverse)
    upper = jnp.floor(middle * (1.0 / 4096.0))
    lower = middle - upper * 4096.0
    code = jnp.clip(jnp.round(x * inverse) - middle, -32767.0, 32767.0)
    code = jnp.where(lane == width, power, code)
    code = jnp.where(lane == width + 1, upper, code)
    code = jnp.where(lane == width + 2, lower, code)
    return code.astype(I32).astype(I16)


def decode(code, width):
    value = code.astype(I32).astype(F32)
    step = jnp.exp2(value[:, width : width + 1])
    middle = value[:, width + 1 : width + 2] * 4096.0 + value[:, width + 2 : width + 3]
    return (value + middle) * step


def logits_kernel(width, row_ref, act_ref, weight_ref, own_ref, right_ref, left_ref, merge_right_ref, merge_left_ref, acc_ref):
    tokens = act_ref.shape[0]
    quarter, half = tokens // 4, tokens // 8
    padded = acc_ref.shape[1]
    tail = padded - 128
    acc_ref[:, tail:padded] = jnp.zeros((tokens, 128), F32)
    act = act_ref[...]
    for start in range(0, width, 512):
        stop = min(start + 512, width)
        acc_ref[:, start:stop] = lax.dot_general(
            act, weight_ref[start:stop, :], (((1,), (1,)), ((), ())), preferred_element_type=F32
        )
    row = row_ref[0]

    def piece(distance, which):
        first = lax.rem(row + distance, 4) * quarter + which * half
        return acc_ref[pl.ds(pl.multiple_of(first, half), half), :]

    own_ref[0:half, :] = piece(0, 0)
    own_ref[half:quarter, :] = piece(0, 1)
    right_ref[0:half, :] = encode(piece(1, 1), width)
    right_ref[half:quarter, :] = encode(piece(2, 0), width)
    left_ref[0:half, :] = encode(piece(3, 0), width)
    left_ref[half:quarter, :] = encode(piece(2, 1), width)
    merge_right_ref[...] = piece(1, 0)
    merge_left_ref[...] = piece(3, 1)


def merge_kernel(width, from_left_ref, from_right_ref, merge_right_ref, merge_left_ref, right_ref, left_ref):
    half = merge_right_ref.shape[0]
    right_ref[...] = encode(merge_right_ref[...] + decode(from_left_ref[half : 2 * half, :], width), width)
    left_ref[...] = encode(merge_left_ref[...] + decode(from_right_ref[half : 2 * half, :], width), width)


def column_to_row(column, offset):
    shape = (column.shape[0], 128)
    here = lax.broadcasted_iota(I32, shape, 0) + offset == lanes_of(shape)
    return jnp.sum(jnp.where(here, column, 0.0), axis=0, keepdims=True)


def row_to_column(row, count, offset):
    shape = (count, 128)
    here = lax.broadcasted_iota(I32, shape, 0) + offset == lanes_of(shape)
    return jnp.sum(jnp.where(here, row, 0.0), axis=1, keepdims=True)


def chunk_of(place_ref, which_chunk):
    core = place_ref[1]
    return core if which_chunk == 0 else 1 - core


def total_kernel(width, which_chunk, place_ref, own_ref, left_one_ref, right_one_ref, left_two_ref, right_two_ref, before_ref, code_ref, stats_ref):
    half, padded = left_two_ref.shape
    offset = chunk_of(place_ref, which_chunk) * (2 * half)
    inside = lanes_of((half, padded)) < width
    peaks, totals = [], []
    for which, one_ref, two_ref in ((0, right_one_ref, left_two_ref), (1, left_one_ref, right_two_ref)):
        rows = slice(which * half, (which + 1) * half)
        logits = own_ref[rows, :] + decode(one_ref[0:half, :], width) + decode(two_ref[...], width)
        logits = jnp.where(inside, logits, -jnp.inf)
        peak = jnp.max(logits, axis=1, keepdims=True)
        weight = jnp.exp(logits - peak)
        code_ref[rows, :] = (jnp.round(weight * CODE_SCALE) - CODE_OFFSET).astype(I32).astype(I16)
        peaks.append(column_to_row(peak, offset + which * half))
        totals.append(column_to_row(jnp.sum(weight, axis=1, keepdims=True), offset + which * half))
    peak, total = peaks[0] + peaks[1], totals[0] + totals[1]
    stats_ref[...] = before_ref[...] + jnp.concatenate([peak, total, jnp.zeros((6, 128), F32)], axis=0)


def teacher_kernel(width, place_ref, ids_ref, values_ref, dense_ref):
    groups, pairs = ids_ref.shape
    tiles = dense_ref.shape[1] // 128
    key_row = lax.broadcasted_iota(I32, (tiles * 8, pairs), 0)
    low_row = lax.broadcasted_iota(I32, (128, pairs), 0)
    token = lax.broadcasted_iota(I32, (1, pairs), 1) // (pairs // 8)
    lane = lax.broadcasted_iota(I32, (8, 128), 1)
    contract = (((1,), (1,)), ((), ()))

    def group(g, _):
        ids = ids_ref[pl.ds(g, 1), :] - place_ref[0]
        value = values_ref[pl.ds(g, 1), :]
        coarse = value.astype(BF16).astype(F32)
        key = lax.shift_right_arithmetic(ids, 7) * 8 + token
        here = key_row == key
        one_hot = jnp.where(low_row == (ids & 127), 1.0, 0.0).astype(BF16)
        dense = lax.dot_general(
            jnp.where(here, coarse, 0.0).astype(BF16), one_hot, contract, preferred_element_type=F32
        )
        dense += lax.dot_general(
            jnp.where(here, value - coarse, 0.0).astype(BF16), one_hot, contract, preferred_element_type=F32
        )
        rows = pl.ds(pl.multiple_of(g * 8, 8), 8)
        for tile in range(tiles):
            block = dense[tile * 8 : tile * 8 + 8, :]
            if tile == tiles - 1:
                block = jnp.where(lane + tile * 128 < width, block, 0.0)
            dense_ref[rows, tile * 128 : tile * 128 + 128] = block
        return 0

    lax.fori_loop(0, groups, group, 0)


def scale_kernel(stats_ref, own_ref, scale_ref):
    peaks = stats_ref[:, 0, :]
    peak = jnp.max(peaks, axis=0, keepdims=True)
    total = jnp.sum(jnp.exp(peaks - peak) * stats_ref[:, 1, :], axis=0, keepdims=True)
    scale = jnp.exp(own_ref[0:1, :] - peak) / total * (LOSS_SCALE / CODE_SCALE)
    scale_ref[...] = jnp.broadcast_to(scale, scale_ref.shape)


def hidden_kernel(
    width, which_chunk, place_ref, own_ref, left_ref, right_ref, left_two_ref, right_two_ref,
    scale_own_ref, scale_left_ref, scale_right_ref, scale_far_ref, dense_ref, weight_ref,
    hidden_ref, grad_ref, last_ref,
):
    quarter, padded = own_ref.shape
    half = quarter // 2
    row, chunk = place_ref[0], chunk_of(place_ref, which_chunk)

    def put(distance, which, code_ref, scale_ref):
        owner = lax.rem(row + distance, 4)
        count = code_ref.shape[0]
        first = pl.multiple_of(owner * quarter + which * half, half)
        token = pl.multiple_of((2 * owner + chunk) * quarter + which * half, half)
        scale = row_to_column(scale_ref[0:1, :], count, chunk * quarter + which * half)
        student = (code_ref[...].astype(I32).astype(F32) + CODE_OFFSET) * scale
        grad = student - LOSS_SCALE * dense_ref[pl.ds(token, count), :]
        grad_ref[pl.ds(first, count), :] = grad.astype(BF16)

    put(0, 0, own_ref, scale_own_ref)
    put(3, 0, left_ref, scale_left_ref)
    put(1, 0, right_ref, scale_right_ref)
    put(2, 0, left_two_ref, scale_far_ref)
    put(2, 1, right_two_ref, scale_far_ref)
    tail = padded - 128
    last_ref[...] = jnp.zeros(last_ref.shape, BF16)
    last_ref[0 : width - tail, :] = weight_ref[tail:width, :]
    total = jnp.dot(grad_ref[:, 0:tail], weight_ref[0:tail, :], preferred_element_type=F32)
    total += jnp.dot(grad_ref[:, tail:padded], last_ref[...], preferred_element_type=F32)
    hidden_ref[...] = total.astype(hidden_ref.dtype)


def weight_kernel(act_a_ref, act_b_ref, grad_a_ref, grad_b_ref, out_ref):
    contract = (((0,), (0,)), ((), ()))
    total = lax.dot_general(grad_a_ref[...], act_a_ref[...], contract, preferred_element_type=F32)
    total += lax.dot_general(grad_b_ref[...], act_b_ref[...], contract, preferred_element_type=F32)
    out_ref[...] = total.astype(BF16)


def pair_kernel(keep_ref, received_ref, sum_ref):
    sum_ref[...] = (keep_ref[...] + received_ref[...]).astype(BF16)


def forward_kernel(a_left_ref, a_right_ref, b_left_ref, b_right_ref, a_first_ref, a_second_ref, b_first_ref, b_second_ref):
    half = a_first_ref.shape[0]
    a_first_ref[...] = a_left_ref[0:half, :]
    a_second_ref[...] = a_right_ref[half : 2 * half, :]
    b_first_ref[...] = b_left_ref[0:half, :]
    b_second_ref[...] = b_right_ref[half : 2 * half, :]


def finish_kernel(part_ref, out_ref):
    out_ref[...] = jnp.sum(part_ref[...].astype(F32), axis=0).astype(BF16)


def shape(dims, dtype):
    return jax.ShapeDtypeStruct(dims, dtype)


def ring(x, step):
    return lax.ppermute(x, "row", [(i, (i + step) % 4) for i in range(4)])


def swap(x):
    return lax.ppermute(x, "core", [(0, 1), (1, 0)])


def local(activations, out_weight, teacher_ids, teacher_values):
    own_tokens, depth = activations.shape
    width = out_weight.shape[1]
    padded = (width + 127) // 128 * 128
    row, core = lax.axis_index("row"), lax.axis_index("core")
    chips = 32
    tokens = chips * own_tokens
    quarter, half = tokens // 4, tokens // 8
    first_col = lax.axis_index(SHARD) * width
    places = jnp.stack([row, core]).astype(I32)

    mine = lax.all_to_all(jnp.broadcast_to(activations[None], (chips, own_tokens, depth)), CHIP, 0, 0)
    mine = mine.reshape(tokens, depth)
    acts = [mine, swap(mine)]
    weight = out_weight.T

    def call(kernel, outs, ins, estimate, scratch=(), after=()):
        count = len(ins)
        ordered = count + len(after)

        def body(*refs):
            kernel(*refs[:count], *refs[ordered:])

        return pl.pallas_call(
            body,
            out_shape=outs,
            in_specs=[SMEM if x.ndim == 1 else VMEM for x in ins] + [pl.BlockSpec(memory_space=pl.ANY)] * len(after),
            out_specs=jax.tree.map(lambda _: VMEM, outs),
            scratch_shapes=scratch,
            compiler_params=PARAMS,
            cost_estimate=estimate,
        )(*ins, *after)

    matmul_flops = 2 * tokens * depth * width
    weight_bytes = depth * padded * 2

    def partial_logits(chunk, after):
        return call(
            functools.partial(logits_kernel, width),
            (
                shape((quarter, padded), F32),
                shape((quarter, padded), I16),
                shape((quarter, padded), I16),
                shape((half, padded), F32),
                shape((half, padded), F32),
            ),
            (places, acts[chunk], weight),
            cost(1, 1),
            [pltpu.VMEM((tokens, padded), F32)],
            after,
        )

    def merge(parts, received, after):
        return call(
            functools.partial(merge_kernel, width),
            (shape((half, padded), I16), shape((half, padded), I16)),
            (*received, parts[3], parts[4]),
            cost(1, 1),
            (),
            after,
        )

    def total(chunk, parts, one, two, before, after):
        return call(
            functools.partial(total_kernel, width, chunk),
            (shape((quarter, padded), I16), shape((8, 128), F32)),
            (places, parts[0], *one, *two, before),
            cost(1, 1),
            (),
            after,
        )

    def hidden(chunk, own, near, far, after):
        return call(
            functools.partial(hidden_kernel, width, chunk),
            (shape((tokens, depth), F32), shape((tokens, padded), BF16)),
            (places, own, *near, *far, *scales, dense, weight),
            cost(1, 1),
            [pltpu.VMEM((128, depth), BF16)],
            after,
        )

    def both_ways(right, left):
        return ring(right, 1), ring(left, 3)

    def all_stats(stats):
        return lax.all_to_all(jnp.broadcast_to(stats[None], (64, 8, 128)), SHARD, 0, 0)

    parts_a = partial_logits(0, ())
    one_a = both_ways(parts_a[1], parts_a[2])
    parts_b = partial_logits(1, parts_a[3:4])
    one_b = both_ways(parts_b[1], parts_b[2])
    merged_a = merge(parts_a, one_a, parts_b[3:4])
    two_a = both_ways(*merged_a)
    merged_b = merge(parts_b, one_b, merged_a[:1])
    two_b = both_ways(*merged_b)
    code_a, stats_a = total(0, parts_a, one_a, two_a, jnp.zeros((8, 128), F32), merged_b[:1])
    near_a = both_ways(code_a, code_a)
    code_b, stats = total(1, parts_b, one_b, two_b, stats_a, (code_a,))
    near_b = both_ways(code_b, code_b)

    pairs = 8 * teacher_ids.shape[1]
    teacher = jax.nn.softmax(teacher_values, axis=1)
    dense = call(
        functools.partial(teacher_kernel, width),
        shape((2 * tokens, padded), F32),
        (jnp.stack([first_col, row]).astype(I32), teacher_ids.reshape(-1, pairs), teacher.reshape(-1, pairs)),
        cost(1, 1),
        (),
        (code_b,),
    )
    scale = call(scale_kernel, shape((8, 128), F32), (all_stats(stats), stats), cost(1, 1), (), (dense,))
    scales = (scale, ring(scale, 1), ring(scale, 3), ring(scale, 2))

    forward = call(
        forward_kernel, (shape((half, padded), I16),) * 4, (*near_a, *near_b), cost(1, 1), (), (scale,)
    )
    far_b = both_ways(forward[2], forward[3])
    far_a = both_ways(forward[0], forward[1])
    hidden_b, full_b = hidden(1, code_b, near_b, far_b, (forward[0],))
    received = swap(hidden_b)
    hidden_a, full_a = hidden(0, code_a, near_a, far_a, (full_b,))
    summed = call(pair_kernel, shape((tokens, depth), BF16), (hidden_a, received), cost(1, 1))
    partial = lax.all_to_all(summed.reshape(chips, own_tokens, depth), CHIP, 0, 0)

    tile = 512
    whole = pl.BlockSpec((tokens, depth), lambda i: (0, 0))
    columns = pl.BlockSpec((tokens, tile), lambda i: (0, i))
    grad_weight = pl.pallas_call(
        weight_kernel,
        out_shape=shape((width, depth), BF16),
        grid=(pl.cdiv(width, tile),),
        in_specs=[whole, whole, columns, columns],
        out_specs=pl.BlockSpec((tile, depth), lambda i: (i, 0)),
        compiler_params=pltpu.CompilerParams(vmem_limit_bytes=58 * 1024 * 1024),
        cost_estimate=cost(2 * matmul_flops, weight_bytes),
    )(acts[0], acts[1], full_a, full_b)

    grad_inputs = call(
        finish_kernel, shape((own_tokens, depth), BF16), (partial,), cost(1, 1), (), (grad_weight,)
    )
    return (grad_inputs, grad_weight.T)


def solution(mesh):
    fine = Mesh(mesh.devices.reshape(4, 4, 2, 2, 4), ("row", "y", "core", "z_lo", "x"))
    specs = (P(SHARD, "row"), P("row", SHARD))
    return jax.shard_map(local, mesh=fine, in_specs=specs + (P(), P()), out_specs=specs, check_vma=False)
```

```python
import functools

import jax
import jax.numpy as jnp
from jax import lax
from jax.experimental import pallas as pl
from jax.experimental.pallas import tpu as pltpu
from jax.sharding import Mesh, PartitionSpec as P

LOSS_SCALE = 64.0
CODE_SCALE = 65535.0
CODE_OFFSET = 32768.0
F32 = jnp.float32
BF16 = jnp.bfloat16
I16 = jnp.int16
I32 = jnp.int32
VMEM = pl.BlockSpec(memory_space=pltpu.VMEM)
SMEM = pl.BlockSpec(memory_space=pltpu.SMEM)
ANY = pl.BlockSpec(memory_space=pl.ANY)
PARAMS = pltpu.CompilerParams(vmem_limit_bytes=20 * 1024 * 1024)
CHIP = ("y", "z_lo", "x")
SHARD = ("y", "core", "z_lo", "x")


def lanes_of(shape):
    return lax.broadcasted_iota(I32, shape, 1)


def encode(x, width):
    lane = lanes_of(x.shape)
    inside = lane < width
    high = jnp.max(jnp.where(inside, x, -jnp.inf), axis=1, keepdims=True)
    low = jnp.min(jnp.where(inside, x, jnp.inf), axis=1, keepdims=True)
    size = jnp.maximum(jnp.abs(high), jnp.abs(low))
    step = jnp.maximum(jnp.maximum((high - low) * (1.0 / 65000.0), size * 2.0**-22), 1e-30)
    power = jnp.ceil(jnp.log2(step))
    inverse = jnp.exp2(-power)
    middle = jnp.round((0.5 * high + 0.5 * low) * inverse)
    upper = jnp.floor(middle * (1.0 / 4096.0))
    lower = middle - upper * 4096.0
    code = jnp.clip(jnp.round(x * inverse) - middle, -32767.0, 32767.0)
    code = jnp.where(lane == width, power, code)
    code = jnp.where(lane == width + 1, upper, code)
    code = jnp.where(lane == width + 2, lower, code)
    return code.astype(I32).astype(I16)


def decode(code, width):
    value = code.astype(I32).astype(F32)
    step = jnp.exp2(value[:, width : width + 1])
    middle = value[:, width + 1 : width + 2] * 4096.0 + value[:, width + 2 : width + 3]
    return (value + middle) * step


def first_logits_kernel(
    width, row_ref, act_ref, rest_ref, weight_hbm, own_ref, right_ref, left_ref, merge_right_ref, merge_left_ref,
    weight_ref, acc_ref, sems,
):
    padded = weight_ref.shape[0]
    rest = rest_ref.shape[0]
    copied = width // rest * rest
    copies = []
    for i, start in enumerate(range(0, copied, 512)):
        rows = pl.ds(start, min(512, copied - start))
        copies.append(pltpu.make_async_copy(weight_hbm.at[rows], weight_ref.at[rows], sems.at[i]))
        copies[-1].start()
    weight_ref[copied : copied + rest, :] = rest_ref[...]
    weight_ref[copied + rest : padded, :] = jnp.zeros((padded - copied - rest, weight_ref.shape[1]), BF16)
    logits_kernel(
        width, row_ref, act_ref, weight_ref, own_ref, right_ref, left_ref, merge_right_ref, merge_left_ref, acc_ref, copies
    )


def logits_kernel(
    width, row_ref, act_ref, weight_ref, own_ref, right_ref, left_ref, merge_right_ref, merge_left_ref, acc_ref, copies=()
):
    tokens = act_ref.shape[0]
    quarter, half = tokens // 4, tokens // 8
    padded = acc_ref.shape[1]
    act = act_ref[...]
    for i, start in enumerate(range(0, padded, 512)):
        stop = min(start + 512, padded)
        if copies:
            copies[i].wait()
        acc_ref[:, start:stop] = lax.dot_general(
            act, weight_ref[start:stop, :], (((1,), (1,)), ((), ())), preferred_element_type=F32
        )
    row = row_ref[0]

    def piece(distance, which):
        first = lax.rem(row + distance, 4) * quarter + which * half
        return acc_ref[pl.ds(pl.multiple_of(first, half), half), :]

    own_ref[0:half, :] = piece(0, 0)
    own_ref[half:quarter, :] = piece(0, 1)
    right_ref[0:half, :] = encode(piece(1, 1), width)
    right_ref[half:quarter, :] = encode(piece(2, 0), width)
    left_ref[0:half, :] = encode(piece(3, 0), width)
    left_ref[half:quarter, :] = encode(piece(2, 1), width)
    merge_right_ref[...] = piece(1, 0)
    merge_left_ref[...] = piece(3, 1)


def merge_kernel(width, from_left_ref, from_right_ref, merge_right_ref, merge_left_ref, right_ref, left_ref):
    half = merge_right_ref.shape[0]
    right_ref[...] = encode(merge_right_ref[...] + decode(from_left_ref[half : 2 * half, :], width), width)
    left_ref[...] = encode(merge_left_ref[...] + decode(from_right_ref[half : 2 * half, :], width), width)


def column_to_row(column, offset):
    shape = (column.shape[0], 128)
    here = lax.broadcasted_iota(I32, shape, 0) + offset == lanes_of(shape)
    return jnp.sum(jnp.where(here, column, 0.0), axis=0, keepdims=True)


def row_to_column(row, count, offset):
    shape = (count, 128)
    here = lax.broadcasted_iota(I32, shape, 0) + offset == lanes_of(shape)
    return jnp.sum(jnp.where(here, row, 0.0), axis=1, keepdims=True)


def chunk_of(place_ref, which_chunk):
    core = place_ref[1]
    return core if which_chunk == 0 else 1 - core


def total_kernel(width, which_chunk, place_ref, own_ref, left_one_ref, right_one_ref, left_two_ref, right_two_ref, before_ref, code_ref, stats_ref):
    half, padded = left_two_ref.shape
    offset = chunk_of(place_ref, which_chunk) * (2 * half)
    inside = lanes_of((half, padded)) < width
    peaks, totals = [], []
    for which, one_ref, two_ref in ((0, right_one_ref, left_two_ref), (1, left_one_ref, right_two_ref)):
        rows = slice(which * half, (which + 1) * half)
        logits = own_ref[rows, :] + decode(one_ref[0:half, :], width) + decode(two_ref[...], width)
        logits = jnp.where(inside, logits, -jnp.inf)
        peak = jnp.max(logits, axis=1, keepdims=True)
        weight = jnp.exp(logits - peak)
        code_ref[rows, :] = (jnp.round(weight * CODE_SCALE) - CODE_OFFSET).astype(I32).astype(I16)
        peaks.append(column_to_row(peak, offset + which * half))
        totals.append(column_to_row(jnp.sum(weight, axis=1, keepdims=True), offset + which * half))
    peak, total = peaks[0] + peaks[1], totals[0] + totals[1]
    stats_ref[...] = before_ref[...] + jnp.concatenate([peak, total, jnp.zeros((6, 128), F32)], axis=0)


def teacher_kernel(width, place_ref, ids_ref, values_ref, dense_ref, teacher_ref):
    tokens, entries = ids_ref.shape
    pairs = 8 * entries
    tiles = dense_ref.shape[1] // 128
    values = values_ref[...]
    weight = jnp.exp(values - jnp.max(values, axis=1, keepdims=True))
    teacher_ref[...] = weight / jnp.sum(weight, axis=1, keepdims=True)
    key_row = lax.broadcasted_iota(I32, (tiles * 8, pairs), 0)
    low_row = lax.broadcasted_iota(I32, (128, pairs), 0)
    token = lax.broadcasted_iota(I32, (1, pairs), 1) // entries
    lane = lax.broadcasted_iota(I32, (8, 128), 1)
    contract = (((1,), (1,)), ((), ()))

    def flat(block):
        return jnp.concatenate([block[n : n + 1, :] for n in range(8)], axis=1)

    def group(g, _):
        rows = pl.ds(pl.multiple_of(g * 8, 8), 8)
        ids = flat(ids_ref[rows, :]) - place_ref[0]
        value = flat(teacher_ref[rows, :])
        coarse = value.astype(BF16).astype(F32)
        key = lax.shift_right_arithmetic(ids, 7) * 8 + token
        here = key_row == key
        one_hot = jnp.where(low_row == (ids & 127), 1.0, 0.0).astype(BF16)
        dense = lax.dot_general(
            jnp.where(here, coarse, 0.0).astype(BF16), one_hot, contract, preferred_element_type=F32
        )
        dense += lax.dot_general(
            jnp.where(here, value - coarse, 0.0).astype(BF16), one_hot, contract, preferred_element_type=F32
        )
        for tile in range(tiles):
            block = dense[tile * 8 : tile * 8 + 8, :]
            if tile == tiles - 1:
                block = jnp.where(lane + tile * 128 < width, block, 0.0)
            dense_ref[rows, tile * 128 : tile * 128 + 128] = block
        return 0

    lax.fori_loop(0, tokens // 8, group, 0, unroll=4)


def pair_stats_kernel(mine_ref, other_ref, out_ref):
    peak_a, peak_b = mine_ref[0:1, :], other_ref[0:1, :]
    peak = jnp.maximum(peak_a, peak_b)
    total = jnp.exp(peak_a - peak) * mine_ref[1:2, :] + jnp.exp(peak_b - peak) * other_ref[1:2, :]
    out_ref[...] = jnp.concatenate([peak, total, jnp.zeros((6, 128), F32)], axis=0)


def scale_kernel(stats_ref, own_ref, scale_ref):
    peaks = stats_ref[:, 0, :]
    peak = jnp.max(peaks, axis=0, keepdims=True)
    total = jnp.sum(jnp.exp(peaks - peak) * stats_ref[:, 1, :], axis=0, keepdims=True)
    scale = jnp.exp(own_ref[0:1, :] - peak) / total * (LOSS_SCALE / CODE_SCALE)
    scale_ref[...] = jnp.broadcast_to(scale, scale_ref.shape)


def grad_rows(code, scale_ref, dense_ref, place_ref, which_chunk, distance, which):
    chunk = chunk_of(place_ref, which_chunk)
    owner = lax.rem(place_ref[0] + distance, 4)
    count = code.shape[0]
    quarter = dense_ref.shape[0] // 8
    first = owner * quarter + which * (quarter // 2)
    token = pl.multiple_of((2 * owner + chunk) * quarter + which * (quarter // 2), quarter // 2)
    scale = row_to_column(scale_ref[0:1, :], count, chunk * quarter + which * (quarter // 2))
    student = (code.astype(I32).astype(F32) + CODE_OFFSET) * scale
    grad = student - LOSS_SCALE * dense_ref[pl.ds(token, count), :]
    return grad.astype(BF16), pl.multiple_of(first, quarter // 2)


def hidden_kernel(
    which_chunk, place_ref, own_ref, left_ref, right_ref, left_two_ref, right_two_ref,
    scale_own_ref, scale_left_ref, scale_right_ref, scale_far_ref, dense_ref, weight_ref, hidden_ref, grad_ref,
):
    half = own_ref.shape[0] // 2
    far = slice(which_chunk * half, (which_chunk + 1) * half)
    for distance, which, code_ref, rows, scale_ref in (
        (0, 0, own_ref, slice(None), scale_own_ref),
        (3, 0, left_ref, slice(None), scale_left_ref),
        (1, 0, right_ref, slice(None), scale_right_ref),
        (2, 0, left_two_ref, far, scale_far_ref),
        (2, 1, right_two_ref, far, scale_far_ref),
    ):
        grad, first = grad_rows(code_ref[rows, :], scale_ref, dense_ref, place_ref, which_chunk, distance, which)
        grad_ref[pl.ds(first, grad.shape[0]), :] = grad
    hidden_ref[...] = jnp.dot(grad_ref[...], weight_ref[...], preferred_element_type=F32)


def weight_kernel(act_a_ref, act_b_ref, grad_a_ref, grad_b_ref, out_ref, token_ref):
    contract = (((0,), (0,)), ((), ()))
    total = lax.dot_general(grad_a_ref[...], act_a_ref[...], contract, preferred_element_type=F32)
    total += lax.dot_general(grad_b_ref[...], act_b_ref[...], contract, preferred_element_type=F32)
    out_ref[...] = total.astype(BF16)
    token_ref[...] = jnp.zeros(token_ref.shape, F32)


def pair_kernel(keep_ref, received_ref, sum_ref):
    sum_ref[...] = (keep_ref[...] + received_ref[...]).astype(BF16)


def forward_kernel(a_left_ref, a_right_ref, b_left_ref, b_right_ref, right_ref, left_ref):
    half = right_ref.shape[0] // 2
    right_ref[0:half, :] = a_left_ref[0:half, :]
    right_ref[half : 2 * half, :] = b_left_ref[0:half, :]
    left_ref[0:half, :] = a_right_ref[half : 2 * half, :]
    left_ref[half : 2 * half, :] = b_right_ref[half : 2 * half, :]


def finish_kernel(part_ref, out_ref):
    out_ref[...] = jnp.sum(part_ref[...].astype(F32), axis=0).astype(BF16)


def pin(x, space=pltpu.VMEM):
    return pltpu.with_memory_space_constraint(x, space)


def ring(x, step):
    return lax.ppermute(x, "row", [(i, (i + step) % 4) for i in range(4)])


def swap(x):
    return lax.ppermute(x, "core", [(0, 1), (1, 0)])


def local(activations, out_weight, teacher_ids, teacher_values):
    own_tokens, depth = activations.shape
    width = out_weight.shape[1]
    padded = (width + 127) // 128 * 128
    row, core = lax.axis_index("row"), lax.axis_index("core")
    chips = 32
    tokens = chips * own_tokens
    quarter, half = tokens // 4, tokens // 8
    first_col = lax.axis_index(SHARD) * width
    places = jnp.stack([row, core]).astype(I32)

    mine = lax.all_to_all(jnp.broadcast_to(activations[None], (chips, own_tokens, depth)), CHIP, 0, 0)
    mine = mine.reshape(tokens, depth)
    acts = [mine, swap(mine)]

    def call(kernel, outs, ins, scratch=(), after=()):
        count, ordered = len(ins), len(ins) + len(after)
        outs = tuple(outs)

        def body(*refs):
            kernel(*refs[:count], *refs[ordered : ordered + len(outs)], *refs[ordered + len(outs) + 1 :])
            refs[ordered + len(outs)][...] = jnp.zeros((8, 128), F32)

        specs = [SMEM if x.ndim == 1 else ANY if x.shape == (width, depth) else VMEM for x in ins]
        ins = [x if x.ndim == 1 else pin(x, pltpu.HBM) if x.shape == (width, depth) else pin(x) for x in ins]
        return pl.pallas_call(
            body,
            out_shape=tuple(pltpu.VMEM(dims, dtype) for dims, dtype in outs) + (pltpu.VMEM((8, 128), F32),),
            in_specs=specs + [ANY] * len(after),
            out_specs=(VMEM,) * (len(outs) + 1),
            scratch_shapes=scratch,
            compiler_params=PARAMS,
            cost_estimate=pl.CostEstimate(flops=1, bytes_accessed=1, transcendentals=0),
        )(*ins, *after)

    def both_ways(right, left):
        return ring(right, 1), ring(left, 3)

    part_outs = (
        ((quarter, padded), F32),
        ((quarter, padded), I16),
        ((quarter, padded), I16),
        ((half, padded), F32),
        ((half, padded), F32),
    )
    acc = pltpu.VMEM((tokens, padded), F32)

    def merge(parts, received, after):
        return call(
            functools.partial(merge_kernel, width),
            (((half, padded), I16), ((half, padded), I16)),
            (*received, parts[3], parts[4]),
            after=after,
        )

    def total(chunk, parts, one, two, before, after):
        return call(
            functools.partial(total_kernel, width, chunk),
            (((quarter, padded), I16), ((8, 128), F32)),
            (places, parts[0], *one, *two, before),
            after=after,
        )

    def hidden(chunk, own, received, after):
        return call(
            functools.partial(hidden_kernel, chunk),
            (((tokens, depth), F32), ((tokens, padded), BF16)),
            (places, own, *received, *codes_far, *scales, dense, weight),
            after=after,
        )

    weight = out_weight.T
    copied = width // 16 * 16
    rest = jnp.pad(weight[copied:], ((0, 16 - (width - copied)), (0, 0)))
    *parts_a, weight, done = call(
        functools.partial(first_logits_kernel, width),
        part_outs + (((padded, depth), BF16),),
        (places, mine, rest, weight),
        (acc, pltpu.SemaphoreType.DMA((8,))),
    )
    one_a = both_ways(parts_a[1], parts_a[2])
    *parts_b, done = call(
        functools.partial(logits_kernel, width), part_outs, (places, acts[1], weight), (acc,), (done,)
    )
    one_b = both_ways(parts_b[1], parts_b[2])
    dense, done = call(
        functools.partial(teacher_kernel, width),
        (((2 * tokens, padded), F32),),
        (jnp.stack([first_col, row]).astype(I32), teacher_ids, teacher_values),
        (pltpu.VMEM(teacher_values.shape, F32),),
        (done,),
    )
    *merged_a, done = merge(parts_a, one_a, (done,))
    two_a = both_ways(*merged_a)
    *merged_b, done = merge(parts_b, one_b, (done,))
    two_b = both_ways(*merged_b)
    code_a, stats, done = total(0, parts_a, one_a, two_a, jnp.zeros((8, 128), F32), (done,))
    near_a = both_ways(code_a, code_a)
    code_b, stats, done = total(1, parts_b, one_b, two_b, stats, (done,))
    near_b = both_ways(code_b, code_b)

    paired, done = call(pair_stats_kernel, (((8, 128), F32),), (stats, swap(stats)), after=(done,))
    gathered = lax.all_to_all(jnp.broadcast_to(paired[None], (chips, 8, 128)), CHIP, 0, 0)
    scale, done = call(scale_kernel, (((8, 128), F32),), (gathered, stats), after=(done,))
    scales = (scale, ring(scale, 1), ring(scale, 3), ring(scale, 2))
    *forward, done = call(
        forward_kernel, (((quarter, padded), I16),) * 2, (*near_a, *near_b), after=(done,)
    )
    codes_far = both_ways(*forward)

    hidden_b, grad_b, done = hidden(1, code_b, near_b, (done,))
    received = swap(hidden_b)
    hidden_a, grad_a, done = hidden(0, code_a, near_a, (done,))
    summed, done = call(pair_kernel, (((tokens, depth), BF16),), (hidden_a, received), after=(done,))
    partial = lax.all_to_all(summed.reshape(chips, own_tokens, depth), CHIP, 0, 0)

    tile = 512
    whole = pl.BlockSpec((tokens, depth), lambda i: (0, 0))
    columns = pl.BlockSpec((tokens, tile), lambda i: (0, i))
    grad_weight, done = pl.pallas_call(
        weight_kernel,
        out_shape=(pltpu.HBM((width, depth), BF16), pltpu.VMEM((8, 128), F32)),
        grid=(pl.cdiv(width, tile),),
        in_specs=[whole, whole, columns, columns],
        out_specs=(pl.BlockSpec((tile, depth), lambda i: (i, 0)), pl.BlockSpec((8, 128), lambda i: (0, 0))),
        compiler_params=PARAMS,
        cost_estimate=pl.CostEstimate(flops=4 * tokens * depth * width, bytes_accessed=1, transcendentals=0),
    )(acts[0], acts[1], grad_a, grad_b)

    grad_inputs, _ = call(finish_kernel, (((own_tokens, depth), BF16),), (partial,), after=(done,))
    return (grad_inputs, grad_weight.T)


def solution(mesh):
    fine = Mesh(mesh.devices.reshape(4, 4, 2, 2, 4), ("row", "y", "core", "z_lo", "x"))
    specs = (P(SHARD, "row"), P("row", SHARD))
    return jax.shard_map(local, mesh=fine, in_specs=specs + (P(), P()), out_specs=specs, check_vma=False)
```

```python
import functools

import jax
import jax.numpy as jnp
from jax import lax
from jax.experimental import pallas as pl
from jax.experimental.pallas import tpu as pltpu
from jax.sharding import Mesh, PartitionSpec as P

LOSS_SCALE = 64.0
CODE_SCALE = 65535.0
CODE_OFFSET = 32768.0
F32 = jnp.float32
BF16 = jnp.bfloat16
I16 = jnp.int16
I32 = jnp.int32
VMEM = pl.BlockSpec(memory_space=pltpu.VMEM)
SMEM = pl.BlockSpec(memory_space=pltpu.SMEM)
ANY = pl.BlockSpec(memory_space=pl.ANY)
PARAMS = pltpu.CompilerParams(vmem_limit_bytes=20 * 1024 * 1024)
CHIP = ("y", "z_lo", "x")
SHARD = ("y", "core", "z_lo", "x")


def lanes_of(shape):
    return lax.broadcasted_iota(I32, shape, 1)


def encode(x, width):
    lane = lanes_of(x.shape)
    inside = lane < width
    high = jnp.max(jnp.where(inside, x, -jnp.inf), axis=1, keepdims=True)
    low = jnp.min(jnp.where(inside, x, jnp.inf), axis=1, keepdims=True)
    size = jnp.maximum(jnp.abs(high), jnp.abs(low))
    step = jnp.maximum(jnp.maximum((high - low) * (1.0 / 65000.0), size * 2.0**-22), 1e-30)
    power = jnp.ceil(jnp.log2(step))
    inverse = jnp.exp2(-power)
    middle = jnp.round((0.5 * high + 0.5 * low) * inverse)
    upper = jnp.floor(middle * (1.0 / 4096.0))
    lower = middle - upper * 4096.0
    code = jnp.clip(jnp.round(x * inverse) - middle, -32767.0, 32767.0)
    code = jnp.where(lane == width, power, code)
    code = jnp.where(lane == width + 1, upper, code)
    code = jnp.where(lane == width + 2, lower, code)
    return code.astype(I32).astype(I16)


def decode(code, width):
    value = code.astype(I32).astype(F32)
    step = jnp.exp2(value[:, width : width + 1])
    middle = value[:, width + 1 : width + 2] * 4096.0 + value[:, width + 2 : width + 3]
    return (value + middle) * step


def first_logits_kernel(
    width, row_ref, act_ref, rest_ref, weight_hbm, own_ref, right_ref, left_ref, merge_right_ref, merge_left_ref,
    weight_ref, acc_ref, sems,
):
    padded = weight_ref.shape[0]
    rest = rest_ref.shape[0]
    copied = width // rest * rest
    copies = []
    for i, start in enumerate(range(0, copied, 512)):
        rows = pl.ds(start, min(512, copied - start))
        copies.append(pltpu.make_async_copy(weight_hbm.at[rows], weight_ref.at[rows], sems.at[i]))
        copies[-1].start()
    weight_ref[copied : copied + rest, :] = rest_ref[...]
    weight_ref[copied + rest : padded, :] = jnp.zeros((padded - copied - rest, weight_ref.shape[1]), BF16)
    logits_kernel(
        width, row_ref, act_ref, weight_ref, own_ref, right_ref, left_ref, merge_right_ref, merge_left_ref, acc_ref, copies
    )


def logits_kernel(
    width, row_ref, act_ref, weight_ref, own_ref, right_ref, left_ref, merge_right_ref, merge_left_ref, acc_ref, copies=()
):
    tokens = act_ref.shape[0]
    quarter, half = tokens // 4, tokens // 8
    padded = acc_ref.shape[1]
    act = act_ref[...]
    for i, start in enumerate(range(0, padded, 512)):
        stop = min(start + 512, padded)
        if copies:
            copies[i].wait()
        acc_ref[:, start:stop] = lax.dot_general(
            act, weight_ref[start:stop, :], (((1,), (1,)), ((), ())), preferred_element_type=F32
        )
    row = row_ref[0]

    def piece(distance, which):
        first = lax.rem(row + distance, 4) * quarter + which * half
        return acc_ref[pl.ds(pl.multiple_of(first, half), half), :]

    own_ref[0:half, :] = piece(0, 0)
    own_ref[half:quarter, :] = piece(0, 1)
    right_ref[0:half, :] = encode(piece(1, 1), width)
    right_ref[half:quarter, :] = encode(piece(2, 0), width)
    left_ref[0:half, :] = encode(piece(3, 0), width)
    left_ref[half:quarter, :] = encode(piece(2, 1), width)
    merge_right_ref[...] = piece(1, 0)
    merge_left_ref[...] = piece(3, 1)


def merge_kernel(width, from_left_ref, from_right_ref, merge_right_ref, merge_left_ref, right_ref, left_ref):
    half = merge_right_ref.shape[0]
    right_ref[...] = encode(merge_right_ref[...] + decode(from_left_ref[half : 2 * half, :], width), width)
    left_ref[...] = encode(merge_left_ref[...] + decode(from_right_ref[half : 2 * half, :], width), width)


def column_to_row(column, offset):
    shape = (column.shape[0], 128)
    here = lax.broadcasted_iota(I32, shape, 0) + offset == lanes_of(shape)
    return jnp.sum(jnp.where(here, column, 0.0), axis=0, keepdims=True)


def row_to_column(row, count, offset):
    shape = (count, 128)
    here = lax.broadcasted_iota(I32, shape, 0) + offset == lanes_of(shape)
    return jnp.sum(jnp.where(here, row, 0.0), axis=1, keepdims=True)


def chunk_of(place_ref, which_chunk):
    core = place_ref[1]
    return core if which_chunk == 0 else 1 - core


def total_kernel(width, which_chunk, place_ref, own_ref, left_one_ref, right_one_ref, left_two_ref, right_two_ref, before_ref, code_ref, stats_ref):
    half, padded = left_two_ref.shape
    offset = chunk_of(place_ref, which_chunk) * (2 * half)
    inside = lanes_of((half, padded)) < width
    peaks, totals = [], []
    for which, one_ref, two_ref in ((0, right_one_ref, left_two_ref), (1, left_one_ref, right_two_ref)):
        rows = slice(which * half, (which + 1) * half)
        logits = own_ref[rows, :] + decode(one_ref[0:half, :], width) + decode(two_ref[...], width)
        logits = jnp.where(inside, logits, -jnp.inf)
        peak = jnp.max(logits, axis=1, keepdims=True)
        weight = jnp.exp(logits - peak)
        code_ref[rows, :] = (jnp.round(weight * CODE_SCALE) - CODE_OFFSET).astype(I32).astype(I16)
        peaks.append(column_to_row(peak, offset + which * half))
        totals.append(column_to_row(jnp.sum(weight, axis=1, keepdims=True), offset + which * half))
    peak, total = peaks[0] + peaks[1], totals[0] + totals[1]
    stats_ref[...] = before_ref[...] + jnp.concatenate([peak, total, jnp.zeros((6, 128), F32)], axis=0)


def teacher_kernel(width, place_ref, ids_ref, values_ref, dense_ref, teacher_ref):
    tokens, entries = ids_ref.shape
    pairs = 8 * entries
    tiles = dense_ref.shape[1] // 128
    values = values_ref[...]
    weight = jnp.exp(values - jnp.max(values, axis=1, keepdims=True))
    teacher_ref[...] = weight / jnp.sum(weight, axis=1, keepdims=True)
    key_row = lax.broadcasted_iota(I32, (tiles * 8, pairs), 0)
    low_row = lax.broadcasted_iota(I32, (128, pairs), 0)
    token = lax.broadcasted_iota(I32, (1, pairs), 1) // entries
    lane = lax.broadcasted_iota(I32, (8, 128), 1)
    contract = (((1,), (1,)), ((), ()))

    def flat(block):
        return jnp.concatenate([block[n : n + 1, :] for n in range(8)], axis=1)

    def group(g, _):
        rows = pl.ds(pl.multiple_of(g * 8, 8), 8)
        ids = flat(ids_ref[rows, :]) - place_ref[0]
        value = flat(teacher_ref[rows, :])
        coarse = value.astype(BF16).astype(F32)
        key = lax.shift_right_arithmetic(ids, 7) * 8 + token
        here = key_row == key
        one_hot = jnp.where(low_row == (ids & 127), 1.0, 0.0).astype(BF16)
        dense = lax.dot_general(
            jnp.where(here, coarse, 0.0).astype(BF16), one_hot, contract, preferred_element_type=F32
        )
        dense += lax.dot_general(
            jnp.where(here, value - coarse, 0.0).astype(BF16), one_hot, contract, preferred_element_type=F32
        )
        for tile in range(tiles):
            block = dense[tile * 8 : tile * 8 + 8, :]
            if tile == tiles - 1:
                block = jnp.where(lane + tile * 128 < width, block, 0.0)
            dense_ref[rows, tile * 128 : tile * 128 + 128] = block
        return 0

    lax.fori_loop(0, tokens // 8, group, 0, unroll=8)


def pair_stats_kernel(mine_ref, other_ref, out_ref):
    peak_a, peak_b = mine_ref[0:1, :], other_ref[0:1, :]
    peak = jnp.maximum(peak_a, peak_b)
    total = jnp.exp(peak_a - peak) * mine_ref[1:2, :] + jnp.exp(peak_b - peak) * other_ref[1:2, :]
    out_ref[...] = jnp.concatenate([peak, total, jnp.zeros((6, 128), F32)], axis=0)


def scale_kernel(stats_ref, own_ref, scale_ref):
    peaks = stats_ref[:, 0, :]
    peak = jnp.max(peaks, axis=0, keepdims=True)
    total = jnp.sum(jnp.exp(peaks - peak) * stats_ref[:, 1, :], axis=0, keepdims=True)
    scale = jnp.exp(own_ref[0:1, :] - peak) / total * (LOSS_SCALE / CODE_SCALE)
    scale_ref[...] = jnp.broadcast_to(scale, scale_ref.shape)


def grad_rows(code, scale_ref, dense_ref, place_ref, which_chunk, distance, which):
    chunk = chunk_of(place_ref, which_chunk)
    owner = lax.rem(place_ref[0] + distance, 4)
    count = code.shape[0]
    quarter = dense_ref.shape[0] // 8
    first = owner * quarter + which * (quarter // 2)
    token = pl.multiple_of((2 * owner + chunk) * quarter + which * (quarter // 2), quarter // 2)
    scale = row_to_column(scale_ref[0:1, :], count, chunk * quarter + which * (quarter // 2))
    student = (code.astype(I32).astype(F32) + CODE_OFFSET) * scale
    grad = student - LOSS_SCALE * dense_ref[pl.ds(token, count), :]
    return grad.astype(BF16), pl.multiple_of(first, quarter // 2)


def hidden_kernel(
    which_chunk, place_ref, own_ref, left_ref, right_ref, left_two_ref, right_two_ref,
    scale_own_ref, scale_left_ref, scale_right_ref, scale_far_ref, dense_ref, weight_ref, hidden_ref, grad_ref,
):
    half = own_ref.shape[0] // 2
    far = slice(which_chunk * half, (which_chunk + 1) * half)
    for distance, which, code_ref, rows, scale_ref in (
        (0, 0, own_ref, slice(None), scale_own_ref),
        (3, 0, left_ref, slice(None), scale_left_ref),
        (1, 0, right_ref, slice(None), scale_right_ref),
        (2, 0, left_two_ref, far, scale_far_ref),
        (2, 1, right_two_ref, far, scale_far_ref),
    ):
        grad, first = grad_rows(code_ref[rows, :], scale_ref, dense_ref, place_ref, which_chunk, distance, which)
        grad_ref[pl.ds(first, grad.shape[0]), :] = grad
    hidden_ref[...] = jnp.dot(grad_ref[...], weight_ref[...], preferred_element_type=F32)


def weight_kernel(act_a_ref, act_b_ref, grad_a_ref, grad_b_ref, out_ref, token_ref):
    contract = (((0,), (0,)), ((), ()))
    total = lax.dot_general(grad_a_ref[...], act_a_ref[...], contract, preferred_element_type=F32)
    total += lax.dot_general(grad_b_ref[...], act_b_ref[...], contract, preferred_element_type=F32)
    out_ref[...] = total.astype(BF16)
    token_ref[...] = jnp.zeros(token_ref.shape, F32)


def pair_kernel(keep_ref, received_ref, sum_ref):
    sum_ref[...] = (keep_ref[...] + received_ref[...]).astype(BF16)


def forward_kernel(a_left_ref, a_right_ref, b_left_ref, b_right_ref, right_ref, left_ref):
    half = right_ref.shape[0] // 2
    right_ref[0:half, :] = a_left_ref[0:half, :]
    right_ref[half : 2 * half, :] = b_left_ref[0:half, :]
    left_ref[0:half, :] = a_right_ref[half : 2 * half, :]
    left_ref[half : 2 * half, :] = b_right_ref[half : 2 * half, :]


def finish_kernel(part_ref, out_ref):
    out_ref[...] = jnp.sum(part_ref[...].astype(F32), axis=0).astype(BF16)


def pin(x, space=pltpu.VMEM):
    return pltpu.with_memory_space_constraint(x, space)


def ring(x, step):
    return lax.ppermute(x, "row", [(i, (i + step) % 4) for i in range(4)])


def swap(x):
    return lax.ppermute(x, "core", [(0, 1), (1, 0)])


def local(activations, out_weight, teacher_ids, teacher_values):
    own_tokens, depth = activations.shape
    width = out_weight.shape[1]
    padded = (width + 127) // 128 * 128
    row, core = lax.axis_index("row"), lax.axis_index("core")
    chips = 32
    tokens = chips * own_tokens
    quarter, half = tokens // 4, tokens // 8
    first_col = lax.axis_index(SHARD) * width
    places = jnp.stack([row, core]).astype(I32)

    mine = lax.all_to_all(jnp.broadcast_to(activations[None], (chips, own_tokens, depth)), CHIP, 0, 0)
    mine = mine.reshape(tokens, depth)
    acts = [mine, swap(mine)]

    def call(kernel, outs, ins, scratch=(), after=(), micros=0):
        count, ordered = len(ins), len(ins) + len(after)
        outs = tuple(outs)

        def body(*refs):
            kernel(*refs[:count], *refs[ordered : ordered + len(outs)], *refs[ordered + len(outs) + 1 :])
            refs[ordered + len(outs)][...] = jnp.zeros((8, 128), F32)

        specs = [SMEM if x.ndim == 1 else ANY if x.shape == (width, depth) else VMEM for x in ins]
        ins = [x if x.ndim == 1 else pin(x, pltpu.HBM) if x.shape == (width, depth) else pin(x) for x in ins]
        return pl.pallas_call(
            body,
            out_shape=tuple((pltpu.HBM if space else pltpu.VMEM)(dims, dtype) for dims, dtype, *space in outs) + (pltpu.VMEM((8, 128), F32),),
            in_specs=specs + [ANY] * len(after),
            out_specs=(VMEM,) * (len(outs) + 1),
            scratch_shapes=scratch,
            compiler_params=PARAMS,
            cost_estimate=pl.CostEstimate(flops=1 + micros * 1_150_000_000, bytes_accessed=1, transcendentals=0),
        )(*ins, *after)

    def both_ways(right, left):
        return ring(right, 1), ring(left, 3)

    part_outs = (
        ((quarter, padded), F32),
        ((quarter, padded), I16),
        ((quarter, padded), I16),
        ((half, padded), F32),
        ((half, padded), F32),
    )
    acc = pltpu.VMEM((tokens, padded), F32)

    def merge(parts, received, after):
        return call(
            functools.partial(merge_kernel, width),
            (((half, padded), I16), ((half, padded), I16)),
            (*received, parts[3], parts[4]),
            after=after,
        )

    def total(chunk, parts, one, two, before, after):
        return call(
            functools.partial(total_kernel, width, chunk),
            (((quarter, padded), I16), ((8, 128), F32)),
            (places, parts[0], *one, *two, before),
            after=after,
        )

    def hidden(chunk, own, received, after):
        return call(
            functools.partial(hidden_kernel, chunk),
            (((tokens, depth), F32), ((tokens, padded), BF16, pltpu.HBM)),
            (places, own, *received, *codes_far, *scales, dense, weight),
            after=after,
        )

    weight = out_weight.T
    copied = width // 16 * 16
    rest = jnp.pad(weight[copied:], ((0, 16 - (width - copied)), (0, 0)))
    *parts_a, weight, done = call(
        functools.partial(first_logits_kernel, width),
        part_outs + (((padded, depth), BF16),),
        (places, mine, rest, weight),
        (acc, pltpu.SemaphoreType.DMA((8,))),
    )
    one_a = both_ways(parts_a[1], parts_a[2])
    *parts_b, done = call(
        functools.partial(logits_kernel, width), part_outs, (places, acts[1], weight), (acc,), (done,)
    )
    one_b = both_ways(parts_b[1], parts_b[2])
    dense, done = call(
        functools.partial(teacher_kernel, width),
        (((2 * tokens, padded), F32),),
        (jnp.stack([first_col, row]).astype(I32), teacher_ids, teacher_values),
        (pltpu.VMEM(teacher_values.shape, F32),),
        (done,),
    )
    *merged_a, done = merge(parts_a, one_a, (done,))
    two_a = both_ways(*merged_a)
    *merged_b, done = merge(parts_b, one_b, (done,))
    two_b = both_ways(*merged_b)
    code_a, stats, done = total(0, parts_a, one_a, two_a, jnp.zeros((8, 128), F32), (done,))
    near_a = both_ways(code_a, code_a)
    code_b, stats, done = total(1, parts_b, one_b, two_b, stats, (done,))
    near_b = both_ways(code_b, code_b)

    paired, done = call(pair_stats_kernel, (((8, 128), F32),), (stats, swap(stats)), after=(done,))
    gathered = lax.all_to_all(jnp.broadcast_to(paired[None], (chips, 8, 128)), CHIP, 0, 0)
    scale, done = call(scale_kernel, (((8, 128), F32),), (gathered, stats), after=(done,))
    scales = (scale, ring(scale, 1), ring(scale, 3), ring(scale, 2))
    *forward, done = call(
        forward_kernel, (((quarter, padded), I16),) * 2, (*near_a, *near_b), after=(done,)
    )
    codes_far = both_ways(*forward)

    hidden_b, grad_b, done = hidden(1, code_b, near_b, (done,))
    received = swap(hidden_b)
    hidden_a, grad_a, done = hidden(0, code_a, near_a, (done,))
    summed, done = call(pair_kernel, (((tokens, depth), BF16),), (hidden_a, received), after=(done,))
    partial = lax.all_to_all(summed.reshape(chips, own_tokens, depth), CHIP, 0, 0)

    tile = 512
    whole = pl.BlockSpec((tokens, depth), lambda i: (0, 0))
    columns = pl.BlockSpec((tokens, tile), lambda i: (0, i))
    grad_weight, done = pl.pallas_call(
        weight_kernel,
        out_shape=(pltpu.HBM((width, depth), BF16), pltpu.VMEM((8, 128), F32)),
        grid=(pl.cdiv(width, tile),),
        in_specs=[whole, whole, columns, columns],
        out_specs=(pl.BlockSpec((tile, depth), lambda i: (i, 0)), pl.BlockSpec((8, 128), lambda i: (0, 0))),
        compiler_params=PARAMS,
        cost_estimate=pl.CostEstimate(flops=4 * tokens * depth * width, bytes_accessed=1, transcendentals=0),
    )(acts[0], acts[1], grad_a, grad_b)

    grad_inputs, _ = call(finish_kernel, (((own_tokens, depth), BF16),), (partial,), after=(done,))
    return (grad_inputs, grad_weight.T)


def solution(mesh):
    fine = Mesh(mesh.devices.reshape(4, 4, 2, 2, 4), ("row", "y", "core", "z_lo", "x"))
    specs = (P(SHARD, "row"), P("row", SHARD))
    return jax.shard_map(local, mesh=fine, in_specs=specs + (P(), P()), out_specs=specs, check_vma=False)
```

```python
import functools

import jax
import jax.numpy as jnp
from jax import lax
from jax.experimental import pallas as pl
from jax.experimental.pallas import tpu as pltpu
from jax.sharding import Mesh, PartitionSpec as P

LOSS_SCALE = 64.0
CODE_SCALE = 65535.0
CODE_OFFSET = 32768.0
F32 = jnp.float32
BF16 = jnp.bfloat16
I16 = jnp.int16
I32 = jnp.int32
VMEM = pl.BlockSpec(memory_space=pltpu.VMEM)
SMEM = pl.BlockSpec(memory_space=pltpu.SMEM)
ANY = pl.BlockSpec(memory_space=pl.ANY)
PARAMS = pltpu.CompilerParams(vmem_limit_bytes=20 * 1024 * 1024)
CHIP = ("y", "z_lo", "x")
SHARD = ("y", "core", "z_lo", "x")


def lanes_of(shape):
    return lax.broadcasted_iota(I32, shape, 1)


def encode(x, width):
    lane = lanes_of(x.shape)
    inside = lane < width
    high = jnp.max(jnp.where(inside, x, -jnp.inf), axis=1, keepdims=True)
    low = jnp.min(jnp.where(inside, x, jnp.inf), axis=1, keepdims=True)
    size = jnp.maximum(jnp.abs(high), jnp.abs(low))
    step = jnp.maximum(jnp.maximum((high - low) * (1.0 / 65000.0), size * 2.0**-22), 1e-30)
    power = jnp.ceil(jnp.log2(step))
    inverse = jnp.exp2(-power)
    middle = jnp.round((0.5 * high + 0.5 * low) * inverse)
    upper = jnp.floor(middle * (1.0 / 4096.0))
    lower = middle - upper * 4096.0
    code = jnp.clip(jnp.round(x * inverse) - middle, -32767.0, 32767.0)
    code = jnp.where(lane == width, power, code)
    code = jnp.where(lane == width + 1, upper, code)
    code = jnp.where(lane == width + 2, lower, code)
    return code.astype(I32).astype(I16)


def decode(code, width):
    value = code.astype(I32).astype(F32)
    step = jnp.exp2(value[:, width : width + 1])
    middle = value[:, width + 1 : width + 2] * 4096.0 + value[:, width + 2 : width + 3]
    return (value + middle) * step


def first_logits_kernel(
    width, row_ref, act_ref, rest_ref, weight_hbm, own_ref, right_ref, left_ref, merge_right_ref, merge_left_ref,
    weight_ref, acc_ref, sems,
):
    padded = weight_ref.shape[0]
    rest = rest_ref.shape[0]
    copied = width // rest * rest
    copies = []
    for i, start in enumerate(range(0, copied, 1024)):
        rows = pl.ds(start, min(1024, copied - start))
        copies.append(pltpu.make_async_copy(weight_hbm.at[rows], weight_ref.at[rows], sems.at[i]))
        copies[-1].start()
    weight_ref[copied : copied + rest, :] = rest_ref[...]
    weight_ref[copied + rest : padded, :] = jnp.zeros((padded - copied - rest, weight_ref.shape[1]), BF16)
    logits_kernel(
        width, row_ref, act_ref, weight_ref, own_ref, right_ref, left_ref, merge_right_ref, merge_left_ref, acc_ref, copies
    )


def logits_kernel(
    width, row_ref, act_ref, weight_ref, own_ref, right_ref, left_ref, merge_right_ref, merge_left_ref, acc_ref, copies=()
):
    tokens = act_ref.shape[0]
    quarter, half = tokens // 4, tokens // 8
    padded = acc_ref.shape[1]
    act = act_ref[...]
    tile = 1024 if copies else 512
    for i, start in enumerate(range(0, padded, tile)):
        stop = min(start + tile, padded)
        if copies:
            copies[i].wait()
        acc_ref[:, start:stop] = lax.dot_general(
            act, weight_ref[start:stop, :], (((1,), (1,)), ((), ())), preferred_element_type=F32
        )
    row = row_ref[0]

    def piece(distance, which):
        first = lax.rem(row + distance, 4) * quarter + which * half
        return acc_ref[pl.ds(pl.multiple_of(first, half), half), :]

    own_ref[0:half, :] = piece(0, 0)
    own_ref[half:quarter, :] = piece(0, 1)
    right_ref[0:half, :] = encode(piece(1, 1), width)
    right_ref[half:quarter, :] = encode(piece(2, 0), width)
    left_ref[0:half, :] = encode(piece(3, 0), width)
    left_ref[half:quarter, :] = encode(piece(2, 1), width)
    merge_right_ref[...] = piece(1, 0)
    merge_left_ref[...] = piece(3, 1)


def merge_kernel(width, from_left_ref, from_right_ref, merge_right_ref, merge_left_ref, right_ref, left_ref):
    half = merge_right_ref.shape[0]
    right_ref[...] = encode(merge_right_ref[...] + decode(from_left_ref[half : 2 * half, :], width), width)
    left_ref[...] = encode(merge_left_ref[...] + decode(from_right_ref[half : 2 * half, :], width), width)


def column_to_row(column, offset):
    shape = (column.shape[0], 128)
    here = lax.broadcasted_iota(I32, shape, 0) + offset == lanes_of(shape)
    return jnp.sum(jnp.where(here, column, 0.0), axis=0, keepdims=True)


def row_to_column(row, count, offset):
    shape = (count, 128)
    here = lax.broadcasted_iota(I32, shape, 0) + offset == lanes_of(shape)
    return jnp.sum(jnp.where(here, row, 0.0), axis=1, keepdims=True)


def chunk_of(place_ref, which_chunk):
    core = place_ref[1]
    return core if which_chunk == 0 else 1 - core


def total_kernel(width, which_chunk, place_ref, own_ref, left_one_ref, right_one_ref, left_two_ref, right_two_ref, before_ref, code_ref, stats_ref):
    half, padded = left_two_ref.shape
    offset = chunk_of(place_ref, which_chunk) * (2 * half)
    inside = lanes_of((half, padded)) < width
    peaks, totals = [], []
    for which, one_ref, two_ref in ((0, right_one_ref, left_two_ref), (1, left_one_ref, right_two_ref)):
        rows = slice(which * half, (which + 1) * half)
        logits = own_ref[rows, :] + decode(one_ref[0:half, :], width) + decode(two_ref[...], width)
        logits = jnp.where(inside, logits, -jnp.inf)
        peak = jnp.max(logits, axis=1, keepdims=True)
        weight = jnp.exp(logits - peak)
        code_ref[rows, :] = (jnp.round(weight * CODE_SCALE) - CODE_OFFSET).astype(I32).astype(I16)
        peaks.append(column_to_row(peak, offset + which * half))
        totals.append(column_to_row(jnp.sum(weight, axis=1, keepdims=True), offset + which * half))
    peak, total = peaks[0] + peaks[1], totals[0] + totals[1]
    stats_ref[...] = before_ref[...] + jnp.concatenate([peak, total, jnp.zeros((6, 128), F32)], axis=0)


def teacher_kernel(width, place_ref, ids_ref, values_ref, dense_ref, teacher_ref):
    tokens, entries = ids_ref.shape
    pairs = 8 * entries
    tiles = dense_ref.shape[1] // 128
    values = values_ref[...]
    weight = jnp.exp(values - jnp.max(values, axis=1, keepdims=True))
    teacher_ref[...] = weight / jnp.sum(weight, axis=1, keepdims=True)
    key_row = lax.broadcasted_iota(I32, (tiles * 8, pairs), 0)
    low_row = lax.broadcasted_iota(I32, (128, pairs), 0)
    token = lax.broadcasted_iota(I32, (1, pairs), 1) // entries
    lane = lax.broadcasted_iota(I32, (8, 128), 1)
    contract = (((1,), (1,)), ((), ()))

    def flat(block):
        return jnp.concatenate([block[n : n + 1, :] for n in range(8)], axis=1)

    def group(g, _):
        rows = pl.ds(pl.multiple_of(g * 8, 8), 8)
        ids = flat(ids_ref[rows, :]) - place_ref[0]
        value = flat(teacher_ref[rows, :])
        coarse = value.astype(BF16).astype(F32)
        key = lax.shift_right_arithmetic(ids, 7) * 8 + token
        here = key_row == key
        one_hot = jnp.where(low_row == (ids & 127), 1.0, 0.0).astype(BF16)
        dense = lax.dot_general(
            jnp.where(here, coarse, 0.0).astype(BF16), one_hot, contract, preferred_element_type=F32
        )
        dense += lax.dot_general(
            jnp.where(here, value - coarse, 0.0).astype(BF16), one_hot, contract, preferred_element_type=F32
        )
        for tile in range(tiles):
            block = dense[tile * 8 : tile * 8 + 8, :]
            if tile == tiles - 1:
                block = jnp.where(lane + tile * 128 < width, block, 0.0)
            dense_ref[rows, tile * 128 : tile * 128 + 128] = block
        return 0

    lax.fori_loop(0, tokens // 8, group, 0, unroll=8)


def pair_stats_kernel(mine_ref, other_ref, out_ref):
    peak_a, peak_b = mine_ref[0:1, :], other_ref[0:1, :]
    peak = jnp.maximum(peak_a, peak_b)
    total = jnp.exp(peak_a - peak) * mine_ref[1:2, :] + jnp.exp(peak_b - peak) * other_ref[1:2, :]
    out_ref[...] = jnp.concatenate([peak, total, jnp.zeros((6, 128), F32)], axis=0)


def scale_kernel(stats_ref, own_ref, scale_ref):
    peaks = stats_ref[:, 0, :]
    peak = jnp.max(peaks, axis=0, keepdims=True)
    total = jnp.sum(jnp.exp(peaks - peak) * stats_ref[:, 1, :], axis=0, keepdims=True)
    scale = jnp.exp(own_ref[0:1, :] - peak) / total * (LOSS_SCALE / CODE_SCALE)
    scale_ref[...] = jnp.broadcast_to(scale, scale_ref.shape)


def grad_rows(code, scale_ref, dense_ref, place_ref, which_chunk, distance, which):
    chunk = chunk_of(place_ref, which_chunk)
    owner = lax.rem(place_ref[0] + distance, 4)
    count = code.shape[0]
    quarter = dense_ref.shape[0] // 8
    first = owner * quarter + which * (quarter // 2)
    token = pl.multiple_of((2 * owner + chunk) * quarter + which * (quarter // 2), quarter // 2)
    scale = row_to_column(scale_ref[0:1, :], count, chunk * quarter + which * (quarter // 2))
    student = (code.astype(I32).astype(F32) + CODE_OFFSET) * scale
    grad = student - LOSS_SCALE * dense_ref[pl.ds(token, count), :]
    return grad.astype(BF16), pl.multiple_of(first, quarter // 2)


def hidden_kernel(
    which_chunk, place_ref, own_ref, left_ref, right_ref, left_two_ref, right_two_ref,
    scale_own_ref, scale_left_ref, scale_right_ref, scale_far_ref, dense_ref, weight_ref, hidden_ref, grad_ref,
):
    half = own_ref.shape[0] // 2
    far = slice(which_chunk * half, (which_chunk + 1) * half)
    for distance, which, code_ref, rows, scale_ref in (
        (0, 0, own_ref, slice(None), scale_own_ref),
        (3, 0, left_ref, slice(None), scale_left_ref),
        (1, 0, right_ref, slice(None), scale_right_ref),
        (2, 0, left_two_ref, far, scale_far_ref),
        (2, 1, right_two_ref, far, scale_far_ref),
    ):
        grad, first = grad_rows(code_ref[rows, :], scale_ref, dense_ref, place_ref, which_chunk, distance, which)
        grad_ref[pl.ds(first, grad.shape[0]), :] = grad
    hidden_ref[...] = jnp.dot(grad_ref[...], weight_ref[...], preferred_element_type=F32)


def weight_kernel(act_a_ref, act_b_ref, grad_a_ref, grad_b_ref, out_ref, token_ref):
    contract = (((0,), (0,)), ((), ()))
    total = lax.dot_general(grad_a_ref[...], act_a_ref[...], contract, preferred_element_type=F32)
    total += lax.dot_general(grad_b_ref[...], act_b_ref[...], contract, preferred_element_type=F32)
    out_ref[...] = total.astype(BF16)
    token_ref[...] = jnp.zeros(token_ref.shape, F32)


def pair_kernel(keep_ref, received_ref, sum_ref):
    sum_ref[...] = (keep_ref[...] + received_ref[...]).astype(BF16)


def forward_kernel(a_left_ref, a_right_ref, b_left_ref, b_right_ref, right_ref, left_ref):
    half = right_ref.shape[0] // 2
    right_ref[0:half, :] = a_left_ref[0:half, :]
    right_ref[half : 2 * half, :] = b_left_ref[0:half, :]
    left_ref[0:half, :] = a_right_ref[half : 2 * half, :]
    left_ref[half : 2 * half, :] = b_right_ref[half : 2 * half, :]


def finish_kernel(part_ref, out_ref):
    out_ref[...] = jnp.sum(part_ref[...].astype(F32), axis=0).astype(BF16)


def pin(x, space=pltpu.VMEM):
    return pltpu.with_memory_space_constraint(x, space)


def ring(x, step):
    return lax.ppermute(x, "row", [(i, (i + step) % 4) for i in range(4)])


def swap(x):
    return lax.ppermute(x, "core", [(0, 1), (1, 0)])


def local(activations, out_weight, teacher_ids, teacher_values):
    own_tokens, depth = activations.shape
    width = out_weight.shape[1]
    padded = (width + 127) // 128 * 128
    row, core = lax.axis_index("row"), lax.axis_index("core")
    chips = 32
    tokens = chips * own_tokens
    quarter, half = tokens // 4, tokens // 8
    first_col = lax.axis_index(SHARD) * width
    places = jnp.stack([row, core]).astype(I32)

    mine = lax.all_to_all(jnp.broadcast_to(activations[None], (chips, own_tokens, depth)), CHIP, 0, 0)
    mine = mine.reshape(tokens, depth)
    acts = [mine, swap(mine)]

    def call(kernel, outs, ins, scratch=(), after=(), micros=0):
        count, ordered = len(ins), len(ins) + len(after)
        outs = tuple(outs)

        def body(*refs):
            kernel(*refs[:count], *refs[ordered : ordered + len(outs)], *refs[ordered + len(outs) + 1 :])
            refs[ordered + len(outs)][...] = jnp.zeros((8, 128), F32)

        specs = [SMEM if x.ndim == 1 else ANY if x.shape == (width, depth) else VMEM for x in ins]
        ins = [x if x.ndim == 1 else pin(x, pltpu.HBM) if x.shape == (width, depth) else pin(x) for x in ins]
        return pl.pallas_call(
            body,
            out_shape=tuple((pltpu.HBM if space else pltpu.VMEM)(dims, dtype) for dims, dtype, *space in outs) + (pltpu.VMEM((8, 128), F32),),
            in_specs=specs + [ANY] * len(after),
            out_specs=(VMEM,) * (len(outs) + 1),
            scratch_shapes=scratch,
            compiler_params=PARAMS,
            cost_estimate=pl.CostEstimate(flops=1 + micros * 1_150_000_000, bytes_accessed=1, transcendentals=0),
        )(*ins, *after)

    def both_ways(right, left):
        return ring(right, 1), ring(left, 3)

    part_outs = (
        ((quarter, padded), F32),
        ((quarter, padded), I16),
        ((quarter, padded), I16),
        ((half, padded), F32),
        ((half, padded), F32),
    )
    acc = pltpu.VMEM((tokens, padded), F32)

    def merge(parts, received, after):
        return call(
            functools.partial(merge_kernel, width),
            (((half, padded), I16), ((half, padded), I16)),
            (*received, parts[3], parts[4]),
            after=after,
        )

    def total(chunk, parts, one, two, before, after):
        return call(
            functools.partial(total_kernel, width, chunk),
            (((quarter, padded), I16), ((8, 128), F32)),
            (places, parts[0], *one, *two, before),
            after=after,
        )

    def hidden(chunk, own, received, after):
        return call(
            functools.partial(hidden_kernel, chunk),
            (((tokens, depth), F32), ((tokens, padded), BF16, pltpu.HBM)),
            (places, own, *received, *codes_far, *scales, dense, weight),
            after=after,
        )

    weight = out_weight.T
    copied = width // 16 * 16
    rest = jnp.pad(weight[copied:], ((0, 16 - (width - copied)), (0, 0)))
    *parts_a, weight, done = call(
        functools.partial(first_logits_kernel, width),
        part_outs + (((padded, depth), BF16),),
        (places, mine, rest, weight),
        (acc, pltpu.SemaphoreType.DMA((3,))),
    )
    one_a = both_ways(parts_a[1], parts_a[2])
    *parts_b, done = call(
        functools.partial(logits_kernel, width), part_outs, (places, acts[1], weight), (acc,), (done,)
    )
    one_b = both_ways(parts_b[1], parts_b[2])
    dense, done = call(
        functools.partial(teacher_kernel, width),
        (((2 * tokens, padded), F32),),
        (jnp.stack([first_col, row]).astype(I32), teacher_ids, teacher_values),
        (pltpu.VMEM(teacher_values.shape, F32),),
        (done,),
    )
    *merged_a, done = merge(parts_a, one_a, (done,))
    two_a = both_ways(*merged_a)
    *merged_b, done = merge(parts_b, one_b, (done,))
    two_b = both_ways(*merged_b)
    code_a, stats, done = total(0, parts_a, one_a, two_a, jnp.zeros((8, 128), F32), (done,))
    near_a = both_ways(code_a, code_a)
    code_b, stats, done = total(1, parts_b, one_b, two_b, stats, (done,))
    near_b = both_ways(code_b, code_b)

    paired, done = call(pair_stats_kernel, (((8, 128), F32),), (stats, swap(stats)), after=(done,))
    gathered = lax.all_to_all(jnp.broadcast_to(paired[None], (chips, 8, 128)), CHIP, 0, 0)
    scale, done = call(scale_kernel, (((8, 128), F32),), (gathered, stats), after=(done,))
    scales = (scale, ring(scale, 1), ring(scale, 3), ring(scale, 2))
    *forward, done = call(
        forward_kernel, (((quarter, padded), I16),) * 2, (*near_a, *near_b), after=(done,)
    )
    codes_far = both_ways(*forward)

    hidden_b, grad_b, done = hidden(1, code_b, near_b, (done,))
    received = swap(hidden_b)
    hidden_a, grad_a, done = hidden(0, code_a, near_a, (done,))
    summed, done = call(pair_kernel, (((tokens, depth), BF16),), (hidden_a, received), after=(done,))
    partial = lax.all_to_all(summed.reshape(chips, own_tokens, depth), CHIP, 0, 0)

    tile = 512
    whole = pl.BlockSpec((tokens, depth), lambda i: (0, 0))
    columns = pl.BlockSpec((tokens, tile), lambda i: (0, i))
    grad_weight, done = pl.pallas_call(
        weight_kernel,
        out_shape=(pltpu.HBM((width, depth), BF16), pltpu.VMEM((8, 128), F32)),
        grid=(pl.cdiv(width, tile),),
        in_specs=[whole, whole, columns, columns],
        out_specs=(pl.BlockSpec((tile, depth), lambda i: (i, 0)), pl.BlockSpec((8, 128), lambda i: (0, 0))),
        compiler_params=PARAMS,
        cost_estimate=pl.CostEstimate(flops=4 * tokens * depth * width, bytes_accessed=1, transcendentals=0),
    )(acts[0], acts[1], grad_a, grad_b)

    grad_inputs, _ = call(finish_kernel, (((own_tokens, depth), BF16),), (partial,), after=(done,))
    return (grad_inputs, grad_weight.T)


def solution(mesh):
    fine = Mesh(mesh.devices.reshape(4, 4, 2, 2, 4), ("row", "y", "core", "z_lo", "x"))
    specs = (P(SHARD, "row"), P("row", SHARD))
    return jax.shard_map(local, mesh=fine, in_specs=specs + (P(), P()), out_specs=specs, check_vma=False)
```

```python
import functools

import jax
import jax.numpy as jnp
from jax import lax
from jax.experimental import pallas as pl
from jax.experimental.pallas import tpu as pltpu
from jax.sharding import Mesh, PartitionSpec as P

LOSS_SCALE = 64.0
CODE_SCALE = 65535.0
CODE_OFFSET = 32768.0
F32 = jnp.float32
BF16 = jnp.bfloat16
I16 = jnp.int16
I32 = jnp.int32
VMEM = pl.BlockSpec(memory_space=pltpu.VMEM)
SMEM = pl.BlockSpec(memory_space=pltpu.SMEM)
ANY = pl.BlockSpec(memory_space=pl.ANY)
PARAMS = pltpu.CompilerParams(vmem_limit_bytes=20 * 1024 * 1024)
CHIP = ("y", "z_lo", "x")
SHARD = ("y", "core", "z_lo", "x")


def lanes_of(shape):
    return lax.broadcasted_iota(I32, shape, 1)


def encode(x, width):
    lane = lanes_of(x.shape)
    inside = lane < width
    high = jnp.max(jnp.where(inside, x, -jnp.inf), axis=1, keepdims=True)
    low = jnp.min(jnp.where(inside, x, jnp.inf), axis=1, keepdims=True)
    size = jnp.maximum(jnp.abs(high), jnp.abs(low))
    step = jnp.maximum(jnp.maximum((high - low) * (1.0 / 65000.0), size * 2.0**-22), 1e-30)
    power = jnp.ceil(jnp.log2(step))
    inverse = jnp.exp2(-power)
    middle = jnp.round((0.5 * high + 0.5 * low) * inverse)
    upper = jnp.floor(middle * (1.0 / 4096.0))
    lower = middle - upper * 4096.0
    code = jnp.clip(jnp.round(x * inverse) - middle, -32767.0, 32767.0)
    code = jnp.where(lane == width, power, code)
    code = jnp.where(lane == width + 1, upper, code)
    code = jnp.where(lane == width + 2, lower, code)
    return code.astype(I32).astype(I16)


def decode(code, width):
    value = code.astype(I32).astype(F32)
    step = jnp.exp2(value[:, width : width + 1])
    middle = value[:, width + 1 : width + 2] * 4096.0 + value[:, width + 2 : width + 3]
    return (value + middle) * step


def first_logits_kernel(
    width, row_ref, act_ref, rest_ref, weight_hbm, own_ref, right_ref, left_ref, merge_right_ref, merge_left_ref,
    weight_ref, acc_ref, sems,
):
    padded = weight_ref.shape[0]
    rest = rest_ref.shape[0]
    copied = width // rest * rest
    copies = []
    for i, start in enumerate(range(0, copied, 512)):
        rows = pl.ds(start, min(512, copied - start))
        copies.append(pltpu.make_async_copy(weight_hbm.at[rows], weight_ref.at[rows], sems.at[i]))
        copies[-1].start()
    weight_ref[copied : copied + rest, :] = rest_ref[...]
    weight_ref[copied + rest : padded, :] = jnp.zeros((padded - copied - rest, weight_ref.shape[1]), BF16)
    logits_kernel(
        width, row_ref, act_ref, weight_ref, own_ref, right_ref, left_ref, merge_right_ref, merge_left_ref, acc_ref, copies
    )


def logits_kernel(
    width, row_ref, act_ref, weight_ref, own_ref, right_ref, left_ref, merge_right_ref, merge_left_ref, acc_ref, copies=()
):
    tokens = act_ref.shape[0]
    quarter, half = tokens // 4, tokens // 8
    padded = acc_ref.shape[1]
    act = act_ref[...]
    for i, start in enumerate(range(0, padded, 512)):
        stop = min(start + 512, padded)
        if copies:
            copies[i].wait()
        acc_ref[:, start:stop] = lax.dot_general(
            act, weight_ref[start:stop, :], (((1,), (1,)), ((), ())), preferred_element_type=F32
        )
    row = row_ref[0]

    def piece(distance, which):
        first = lax.rem(row + distance, 4) * quarter + which * half
        return acc_ref[pl.ds(pl.multiple_of(first, half), half), :]

    own_ref[0:half, :] = piece(0, 0)
    own_ref[half:quarter, :] = piece(0, 1)
    right_ref[0:half, :] = encode(piece(1, 1), width)
    right_ref[half:quarter, :] = encode(piece(2, 0), width)
    left_ref[0:half, :] = encode(piece(3, 0), width)
    left_ref[half:quarter, :] = encode(piece(2, 1), width)
    merge_right_ref[...] = piece(1, 0)
    merge_left_ref[...] = piece(3, 1)


def merge_kernel(width, from_left_ref, from_right_ref, merge_right_ref, merge_left_ref, right_ref, left_ref):
    half = merge_right_ref.shape[0]
    right_ref[...] = encode(merge_right_ref[...] + decode(from_left_ref[half : 2 * half, :], width), width)
    left_ref[...] = encode(merge_left_ref[...] + decode(from_right_ref[half : 2 * half, :], width), width)


def column_to_row(column, offset):
    shape = (column.shape[0], 128)
    here = lax.broadcasted_iota(I32, shape, 0) + offset == lanes_of(shape)
    return jnp.sum(jnp.where(here, column, 0.0), axis=0, keepdims=True)


def row_to_column(row, count, offset):
    shape = (count, 128)
    here = lax.broadcasted_iota(I32, shape, 0) + offset == lanes_of(shape)
    return jnp.sum(jnp.where(here, row, 0.0), axis=1, keepdims=True)


def chunk_of(place_ref, which_chunk):
    core = place_ref[1]
    return core if which_chunk == 0 else 1 - core


def total_kernel(width, which_chunk, place_ref, own_ref, left_one_ref, right_one_ref, left_two_ref, right_two_ref, before_ref, code_ref, stats_ref):
    half, padded = left_two_ref.shape
    offset = chunk_of(place_ref, which_chunk) * (2 * half)
    inside = lanes_of((half, padded)) < width
    peaks, totals = [], []
    for which, one_ref, two_ref in ((0, right_one_ref, left_two_ref), (1, left_one_ref, right_two_ref)):
        rows = slice(which * half, (which + 1) * half)
        logits = own_ref[rows, :] + decode(one_ref[0:half, :], width) + decode(two_ref[...], width)
        logits = jnp.where(inside, logits, -jnp.inf)
        peak = jnp.max(logits, axis=1, keepdims=True)
        weight = jnp.exp(logits - peak)
        code_ref[rows, :] = (jnp.round(weight * CODE_SCALE) - CODE_OFFSET).astype(I32).astype(I16)
        peaks.append(column_to_row(peak, offset + which * half))
        totals.append(column_to_row(jnp.sum(weight, axis=1, keepdims=True), offset + which * half))
    peak, total = peaks[0] + peaks[1], totals[0] + totals[1]
    stats_ref[...] = before_ref[...] + jnp.concatenate([peak, total, jnp.zeros((6, 128), F32)], axis=0)


def teacher_kernel(width, place_ref, ids_ref, values_ref, dense_ref, teacher_ref):
    tokens, entries = ids_ref.shape
    pairs = 8 * entries
    tiles = dense_ref.shape[1] // 128
    values = values_ref[...]
    weight = jnp.exp(values - jnp.max(values, axis=1, keepdims=True))
    teacher_ref[...] = weight / jnp.sum(weight, axis=1, keepdims=True)
    key_row = lax.broadcasted_iota(I32, (tiles * 8, pairs), 0)
    low_row = lax.broadcasted_iota(I32, (128, pairs), 0)
    token = lax.broadcasted_iota(I32, (1, pairs), 1) // entries
    lane = lax.broadcasted_iota(I32, (8, 128), 1)
    contract = (((1,), (1,)), ((), ()))

    def flat(block):
        return jnp.concatenate([block[n : n + 1, :] for n in range(8)], axis=1)

    def group(g, _):
        source = (2 * (g // 8) + place_ref[1]) * 64 + (g % 8) * 8
        rows = pl.ds(pl.multiple_of(source, 8), 8)
        ids = flat(ids_ref[rows, :]) - place_ref[0]
        value = flat(teacher_ref[rows, :])
        coarse = value.astype(BF16).astype(F32)
        key = lax.shift_right_arithmetic(ids, 7) * 8 + token
        here = key_row == key
        one_hot = jnp.where(low_row == (ids & 127), 1.0, 0.0).astype(BF16)
        dense = lax.dot_general(
            jnp.where(here, coarse, 0.0).astype(BF16), one_hot, contract, preferred_element_type=F32
        )
        dense += lax.dot_general(
            jnp.where(here, value - coarse, 0.0).astype(BF16), one_hot, contract, preferred_element_type=F32
        )
        rows = pl.ds(pl.multiple_of(g * 8, 8), 8)
        for tile in range(tiles):
            block = dense[tile * 8 : tile * 8 + 8, :]
            if tile == tiles - 1:
                block = jnp.where(lane + tile * 128 < width, block, 0.0)
            dense_ref[rows, tile * 128 : tile * 128 + 128] = block
        return 0

    lax.fori_loop(0, dense_ref.shape[0] // 8, group, 0, unroll=8)


def pair_stats_kernel(mine_ref, other_ref, out_ref):
    peak_a, peak_b = mine_ref[0:1, :], other_ref[0:1, :]
    peak = jnp.maximum(peak_a, peak_b)
    total = jnp.exp(peak_a - peak) * mine_ref[1:2, :] + jnp.exp(peak_b - peak) * other_ref[1:2, :]
    out_ref[...] = jnp.concatenate([peak, total, jnp.zeros((6, 128), F32)], axis=0)


def scale_kernel(stats_ref, own_ref, scale_ref):
    peaks = stats_ref[:, 0, :]
    peak = jnp.max(peaks, axis=0, keepdims=True)
    total = jnp.sum(jnp.exp(peaks - peak) * stats_ref[:, 1, :], axis=0, keepdims=True)
    scale = jnp.exp(own_ref[0:1, :] - peak) / total * (LOSS_SCALE / CODE_SCALE)
    scale_ref[...] = jnp.broadcast_to(scale, scale_ref.shape)


def grad_rows(code, scale_ref, dense_ref, place_ref, which_chunk, distance, which):
    chunk = chunk_of(place_ref, which_chunk)
    owner = lax.rem(place_ref[0] + distance, 4)
    count = code.shape[0]
    quarter = dense_ref.shape[0] // 4
    first = owner * quarter + which * (quarter // 2)
    first = pl.multiple_of(first, quarter // 2)
    scale = row_to_column(scale_ref[0:1, :], count, chunk * quarter + which * (quarter // 2))
    student = (code.astype(I32).astype(F32) + CODE_OFFSET) * scale
    grad = student - LOSS_SCALE * dense_ref[pl.ds(first, count), :]
    return grad.astype(BF16), first


def hidden_kernel(
    which_chunk, place_ref, own_ref, left_ref, right_ref, left_two_ref, right_two_ref,
    scale_own_ref, scale_left_ref, scale_right_ref, scale_far_ref, dense_ref, weight_ref, hidden_ref, grad_ref,
):
    half = own_ref.shape[0] // 2
    far = slice(which_chunk * half, (which_chunk + 1) * half)
    for distance, which, code_ref, rows, scale_ref in (
        (0, 0, own_ref, slice(None), scale_own_ref),
        (3, 0, left_ref, slice(None), scale_left_ref),
        (1, 0, right_ref, slice(None), scale_right_ref),
        (2, 0, left_two_ref, far, scale_far_ref),
        (2, 1, right_two_ref, far, scale_far_ref),
    ):
        grad, first = grad_rows(code_ref[rows, :], scale_ref, dense_ref, place_ref, which_chunk, distance, which)
        grad_ref[pl.ds(first, grad.shape[0]), :] = grad
    hidden_ref[...] = jnp.dot(grad_ref[...], weight_ref[...], preferred_element_type=F32)


def weight_kernel(act_a_ref, act_b_ref, grad_a_ref, grad_b_ref, out_ref, token_ref):
    contract = (((0,), (0,)), ((), ()))
    total = lax.dot_general(grad_a_ref[...], act_a_ref[...], contract, preferred_element_type=F32)
    total += lax.dot_general(grad_b_ref[...], act_b_ref[...], contract, preferred_element_type=F32)
    out_ref[...] = total.astype(BF16)
    token_ref[...] = jnp.zeros(token_ref.shape, F32)


def pair_kernel(keep_ref, received_ref, sum_ref):
    sum_ref[...] = (keep_ref[...] + received_ref[...]).astype(BF16)


def forward_kernel(a_left_ref, a_right_ref, b_left_ref, b_right_ref, right_ref, left_ref):
    half = right_ref.shape[0] // 2
    right_ref[0:half, :] = a_left_ref[0:half, :]
    right_ref[half : 2 * half, :] = b_left_ref[0:half, :]
    left_ref[0:half, :] = a_right_ref[half : 2 * half, :]
    left_ref[half : 2 * half, :] = b_right_ref[half : 2 * half, :]


def finish_kernel(part_ref, out_ref):
    out_ref[...] = jnp.sum(part_ref[...].astype(F32), axis=0).astype(BF16)


def pin(x, space=pltpu.VMEM):
    return pltpu.with_memory_space_constraint(x, space)


def ring(x, step):
    return lax.ppermute(x, "row", [(i, (i + step) % 4) for i in range(4)])


def swap(x):
    return lax.ppermute(x, "core", [(0, 1), (1, 0)])


def local(activations, out_weight, teacher_ids, teacher_values):
    own_tokens, depth = activations.shape
    width = out_weight.shape[1]
    padded = (width + 127) // 128 * 128
    row, core = lax.axis_index("row"), lax.axis_index("core")
    chips = 32
    tokens = chips * own_tokens
    quarter, half = tokens // 4, tokens // 8
    first_col = lax.axis_index(SHARD) * width
    places = jnp.stack([row, core]).astype(I32)

    mine = lax.all_to_all(jnp.broadcast_to(activations[None], (chips, own_tokens, depth)), CHIP, 0, 0)
    mine = mine.reshape(tokens, depth)
    acts = [mine, swap(mine)]

    def call(kernel, outs, ins, scratch=(), after=(), micros=0):
        count, ordered = len(ins), len(ins) + len(after)
        outs = tuple(outs)

        def body(*refs):
            kernel(*refs[:count], *refs[ordered : ordered + len(outs)], *refs[ordered + len(outs) + 1 :])
            refs[ordered + len(outs)][...] = jnp.zeros((8, 128), F32)

        specs = [SMEM if x.ndim == 1 else ANY if x.shape == (width, depth) else VMEM for x in ins]
        ins = [x if x.ndim == 1 else pin(x, pltpu.HBM) if x.shape == (width, depth) else pin(x) for x in ins]
        return pl.pallas_call(
            body,
            out_shape=tuple((pltpu.HBM if space else pltpu.VMEM)(dims, dtype) for dims, dtype, *space in outs) + (pltpu.VMEM((8, 128), F32),),
            in_specs=specs + [ANY] * len(after),
            out_specs=(VMEM,) * (len(outs) + 1),
            scratch_shapes=scratch,
            compiler_params=PARAMS,
            cost_estimate=pl.CostEstimate(flops=1 + micros * 1_150_000_000, bytes_accessed=1, transcendentals=0),
        )(*ins, *after)

    def both_ways(right, left):
        return ring(right, 1), ring(left, 3)

    part_outs = (
        ((quarter, padded), F32),
        ((quarter, padded), I16),
        ((quarter, padded), I16),
        ((half, padded), F32),
        ((half, padded), F32),
    )
    acc = pltpu.VMEM((tokens, padded), F32)

    def merge(parts, received, after):
        return call(
            functools.partial(merge_kernel, width),
            (((half, padded), I16), ((half, padded), I16)),
            (*received, parts[3], parts[4]),
            after=after,
        )

    def total(chunk, parts, one, two, before, after):
        return call(
            functools.partial(total_kernel, width, chunk),
            (((quarter, padded), I16), ((8, 128), F32)),
            (places, parts[0], *one, *two, before),
            after=after,
        )

    def hidden(chunk, own, received, after):
        return call(
            functools.partial(hidden_kernel, chunk),
            (((tokens, depth), F32), ((tokens, padded), BF16, pltpu.HBM)),
            (places, own, *received, *codes_far, *scales, (dense_a, dense_b)[chunk], weight),
            after=after,
        )

    weight = out_weight.T
    copied = width // 16 * 16
    rest = jnp.pad(weight[copied:], ((0, 16 - (width - copied)), (0, 0)))
    *parts_a, weight, done = call(
        functools.partial(first_logits_kernel, width),
        part_outs + (((padded, depth), BF16),),
        (places, mine, rest, weight),
        (acc, pltpu.SemaphoreType.DMA((8,))),
    )
    one_a = both_ways(parts_a[1], parts_a[2])
    *parts_b, done = call(
        functools.partial(logits_kernel, width), part_outs, (places, acts[1], weight), (acc,), (done,)
    )
    one_b = both_ways(parts_b[1], parts_b[2])
    def teacher(chunk, after):
        return call(
            functools.partial(teacher_kernel, width),
            (((tokens, padded), F32),),
            (jnp.stack([first_col, chunk]).astype(I32), teacher_ids, teacher_values),
            (pltpu.VMEM(teacher_values.shape, F32),),
            after,
        )

    dense_b, done = teacher(1 - core, (done,))
    *merged_a, done = merge(parts_a, one_a, (done,))
    two_a = both_ways(*merged_a)
    dense_a, done = teacher(core, (done,))
    *merged_b, done = merge(parts_b, one_b, (done,))
    two_b = both_ways(*merged_b)
    code_a, stats, done = total(0, parts_a, one_a, two_a, jnp.zeros((8, 128), F32), (done,))
    near_a = both_ways(code_a, code_a)
    code_b, stats, done = total(1, parts_b, one_b, two_b, stats, (done,))
    near_b = both_ways(code_b, code_b)

    paired, done = call(pair_stats_kernel, (((8, 128), F32),), (stats, swap(stats)), after=(done,))
    gathered = lax.all_to_all(jnp.broadcast_to(paired[None], (chips, 8, 128)), CHIP, 0, 0)
    scale, done = call(scale_kernel, (((8, 128), F32),), (gathered, stats), after=(done,))
    scales = (scale, ring(scale, 1), ring(scale, 3), ring(scale, 2))
    *forward, done = call(
        forward_kernel, (((quarter, padded), I16),) * 2, (*near_a, *near_b), after=(done,)
    )
    codes_far = both_ways(*forward)

    hidden_b, grad_b, done = hidden(1, code_b, near_b, (done,))
    received = swap(hidden_b)
    hidden_a, grad_a, done = hidden(0, code_a, near_a, (done,))
    summed, done = call(pair_kernel, (((tokens, depth), BF16),), (hidden_a, received), after=(done,))
    partial = lax.all_to_all(summed.reshape(chips, own_tokens, depth), CHIP, 0, 0)

    tile = 512
    whole = pl.BlockSpec((tokens, depth), lambda i: (0, 0))
    columns = pl.BlockSpec((tokens, tile), lambda i: (0, i))
    grad_weight, done = pl.pallas_call(
        weight_kernel,
        out_shape=(pltpu.HBM((width, depth), BF16), pltpu.VMEM((8, 128), F32)),
        grid=(pl.cdiv(width, tile),),
        in_specs=[whole, whole, columns, columns],
        out_specs=(pl.BlockSpec((tile, depth), lambda i: (i, 0)), pl.BlockSpec((8, 128), lambda i: (0, 0))),
        compiler_params=PARAMS,
        cost_estimate=pl.CostEstimate(flops=4 * tokens * depth * width, bytes_accessed=1, transcendentals=0),
    )(acts[0], acts[1], grad_a, grad_b)

    grad_inputs, _ = call(finish_kernel, (((own_tokens, depth), BF16),), (partial,), after=(done,))
    return (grad_inputs, grad_weight.T)


def solution(mesh):
    fine = Mesh(mesh.devices.reshape(4, 4, 2, 2, 4), ("row", "y", "core", "z_lo", "x"))
    specs = (P(SHARD, "row"), P("row", SHARD))
    return jax.shard_map(local, mesh=fine, in_specs=specs + (P(), P()), out_specs=specs, check_vma=False)
```
